128 devices in a mesh: ctx: 16 (over x_hi, z, core), mp: 8 (over x_lo, y).
Axes of the slice: x: 4 (x_hi: 2, x_lo: 2; x = x_hi * 2 + x_lo), y: 4, z: 4, core: 2. Of those that a mesh axis runs over, the one named last changes fastest.
Arguments:
- tokens: bfloat16 [2048, 4096], P('ctx'), may hold values from -8 to 8
- out_grad: bfloat16 [2048, 4096], P('ctx'), may hold values from -8 to 8
- in_weight: bfloat16 [4096, 3, 4096], P(None, None, 'mp'), may hold values from -0.09375 to 0.09375
- out_weight: bfloat16 [4096, 4096], P('mp'), may hold values from -0.09375 to 0.09375
- filters: float32 [2048, 4096], P('ctx', 'mp'), may hold values from -0.125 to 0.125
Outputs:
- input_grad: bfloat16 [2048, 4096], P('ctx', 'mp')
- in_weight_grad: float32 [4096, 3, 4096], P('ctx', None, 'mp')
- out_weight_grad: float32 [4096, 4096], P('mp', 'ctx')
- filter_grad: float32 [2048, 4096], P('ctx', 'mp')
The draws below stay inside these ranges and needn't reach their ends.
All inputs are finite; a program needn't handle non-finite values.
Results may differ from the reference program's by a relative error of at most 0.025.
Values may be sent and summed in bfloat16 or wider, within the bound.
No kernel may reach another device: no remote copies, remote signals or barrier semaphores. Data moves between devices by JAX's collectives and lax.ppermute only.
A program may use at most 192 MiB of HBM per device.

```python
import math
import jax
import jax.numpy as jnp
from jax import lax

D = 4096
C = 4096
SEQ_DEV = 128
SEQ = 2048
N_CTX = 16


def spiked(values, stream_key, source, target, shards_of, factor):
    owner, partner = [(jnp.arange(values.shape[axis_at]) // (values.shape[axis_at] // shards_of)).reshape([-1 if axis == axis_at else 1 for axis in range(values.ndim)]) for axis_at in (source, target)]
    chosen = jax.random.permutation(stream_key, shards_of)[partner]
    strong = (owner == chosen) | (owner == (partner + shards_of // 2) % shards_of)
    return jnp.where(strong, factor * values, values)


def shard_levels(stream_key, shape, shards, least, largest):
    level = 1.0
    for dim, parts in shards:
        steps = jax.random.uniform(jax.random.fold_in(jax.random.fold_in(stream_key, 6), dim), (parts,), jnp.float32, least / len(shards), largest / len(shards))
        level = level * jnp.repeat(jnp.exp(steps), shape[dim] // parts).reshape((-1,) + (1,) * (len(shape) - 1 - dim))
    return level


def noise(rng, extent, scale, limit, shards=(), dtype=jnp.bfloat16):
    values = jax.random.normal(rng, extent, jnp.float32) * scale
    if len(shards) > 0:
        values = shard_levels(rng, extent, shards, -0.22, 0.18) * values
    return jnp.clip(values, min=-limit, max=limit).astype(dtype)


def gaussian_with(own_key, dims, scale, bound, cuts, heavy, held_as=jnp.bfloat16):
    values = scale * jax.random.normal(own_key, dims, jnp.float32)
    if cuts:
        values = values * shard_levels(own_key, dims, cuts, -0.22, 0.18)
    return jnp.clip(spiked(values, jax.random.fold_in(own_key, 3), *heavy), -bound, bound).astype(held_as)


def setup_inputs(seed: int = 0) -> dict:
    streams_of = jax.random.split(jax.random.key(seed), 6)
    return {
        "tokens": gaussian_with(streams_of[0], (SEQ, D), 1.0, 8.0, ((0, 16),), (0, 1, 16, 2.0)),
        "out_grad": gaussian_with(streams_of[1], (SEQ, D), 1.0, 8.0, ((0, 16),), (0, 1, 16, 2.0)),
        "in_weight": noise(streams_of[2], (D, 3, C), D ** -0.5, 0.09375, ((2, 8),)),
        "out_weight": noise(streams_of[3], (C, D), C ** -0.5, 0.09375, ((0, 8),)),
        "filters": noise(streams_of[4], (SEQ, C), (SEQ ** -0.5), 0.125, ((0, 16), (1, 8)), jnp.float32),
    }


def spectrum(signal):
    return jnp.fft.rfft(signal, n=2 * SEQ, axis=0)

def restore(values):
    return jnp.fft.irfft(values, n=2 * SEQ, axis=0)[:SEQ].astype(jnp.float32)

def reference(tokens, out_grad, in_weight, out_weight, filters):
    flat_weight = in_weight.reshape(D, 3 * C)
    project = jnp.dot(tokens, flat_weight, preferred_element_type=jnp.float32).astype(jnp.bfloat16).reshape(SEQ, 3, C)
    query = project[:, 0].astype(jnp.float32)
    key_part = project[:, 1].astype(jnp.float32)
    value = project[:, 2].astype(jnp.float32)
    mixed = key_part * value
    filt_spec = spectrum(filters)
    mix_spec = spectrum(mixed)
    conv_out = restore(filt_spec * mix_spec)
    gated = (query * conv_out).astype(jnp.bfloat16)
    grad_gate = jnp.dot(out_grad, out_weight.T, preferred_element_type=jnp.float32)
    grad_query = grad_gate * conv_out
    grad_conv = grad_gate * query
    conv_spec = spectrum(grad_conv)
    grad_mixed = restore(jnp.conj(filt_spec) * conv_spec)
    raw_filter = restore(jnp.conj(mix_spec) * conv_spec)
    grad_key = grad_mixed * value
    grad_value = grad_mixed * key_part
    grads = jnp.stack([grad_query, grad_key, grad_value], axis=1).astype(jnp.bfloat16)
    flat_grads = grads.reshape(SEQ, 3 * C)
    input_grad = jnp.dot(flat_grads, flat_weight.T, preferred_element_type=jnp.float32).astype(jnp.bfloat16)

    def add_block(index, sums):
        start = (index * SEQ_DEV).astype(jnp.int32)
        token_rows = lax.dynamic_slice_in_dim(tokens, start, SEQ_DEV, 0)
        grad_rows = lax.dynamic_slice_in_dim(flat_grads, start, SEQ_DEV, 0)
        gate_rows = lax.dynamic_slice_in_dim(gated, start, SEQ_DEV, 0)
        cot_rows = lax.dynamic_slice_in_dim(out_grad, start, SEQ_DEV, 0)
        in_part = jnp.dot(token_rows.T, grad_rows, preferred_element_type=jnp.float32)
        out_part = jnp.dot(gate_rows.T, cot_rows, preferred_element_type=jnp.float32)
        in_part = lax.optimization_barrier(in_part.astype(jnp.bfloat16)).astype(jnp.float32)
        out_part = lax.optimization_barrier(out_part.astype(jnp.bfloat16)).astype(jnp.float32)
        return (sums[0] + in_part, sums[1] + out_part)
    start_sums = (jnp.zeros((D, 3 * C), jnp.float32), jnp.zeros((C, D), jnp.float32))
    in_sum, out_sum = lax.fori_loop(0, N_CTX, add_block, start_sums)
    factor = 1.0 / math.sqrt(SEQ)
    return (input_grad, (in_sum * factor).reshape(D, 3, C), out_sum * factor, raw_filter * factor)
```

```python
import math

import jax
import jax.numpy as jnp
import ml_dtypes
import numpy as np
from jax import lax
from jax.experimental import pallas as pl
from jax.experimental.pallas import tpu as pltpu
from jax.sharding import PartitionSpec as P

F32 = jnp.float32
BF16 = jnp.bfloat16
NT = (((1,), (1,)), ((), ()))
NN = (((1,), (0,)), ((), ()))
MIB = 1 << 20
BLOCK = 32
SEQ_DEV = 128
SEQ = 2048


def dot(a, b, dims=NN):
    return lax.dot_general(a, b, dims, preferred_element_type=F32)


def call(kernel, *, flops=0, bytes_accessed=0, vmem=32, **kw):
    return pl.pallas_call(
        kernel,
        compiler_params=pltpu.CompilerParams(vmem_limit_bytes=vmem * MIB),
        cost_estimate=pl.CostEstimate(flops=flops, bytes_accessed=bytes_accessed, transcendentals=0),
        **kw,
    )


def split_columns(tokens, out_grad):
    def kernel(t_ref, g_ref, o_ref):
        for p in range(4):
            for h in range(2):
                lanes = pl.ds(p * 256 + h * 128, 128)
                o_ref[p, pl.ds(h * 128, 128), :] = t_ref[:, lanes]
                o_ref[p, pl.ds(256 + h * 128, 128), :] = g_ref[:, lanes]

    spec = pl.BlockSpec((SEQ_DEV, 1024), lambda s: (0, s))
    return call(
        kernel,
        grid=(4,),
        in_specs=[spec, spec],
        out_specs=pl.BlockSpec((4, 512, 128), lambda s: (s, 0, 0)),
        out_shape=jax.ShapeDtypeStruct((16, 512, 128), BF16),
        bytes_accessed=4 * MIB,
        name="split_columns",
    )(tokens, out_grad)


def project(tokens, out_grad, weight, out_weight, filters):
    def kernel(t_ref, g_ref, w_ref, ow_ref, f_ref, o_ref):
        s = pl.program_id(0)

        def put(rows):
            o_ref[...] = rows.astype(BF16).reshape(8, 1, BLOCK, SEQ_DEV)

        @pl.when(s < 6)
        def _():
            put(dot(t_ref[...], w_ref[0]).T)

        @pl.when((s >= 6) & (s < 8))
        def _():
            put(dot(ow_ref[...], g_ref[...], NT))

        @pl.when(s >= 8)
        def _():
            put(f_ref[...].T)

    def w_map(s):
        s = jnp.minimum(s, 5)
        return (s // 2, 0, s % 2)

    return call(
        kernel,
        grid=(10,),
        in_specs=[
            pl.BlockSpec((SEQ_DEV, 4096), lambda s: (0, 0)),
            pl.BlockSpec((SEQ_DEV, 4096), lambda s: (0, 0)),
            pl.BlockSpec((1, 4096, 256), w_map),
            pl.BlockSpec((256, 4096), lambda s: (jnp.clip(s - 6, 0, 1), 0)),
            pl.BlockSpec((SEQ_DEV, 256), lambda s: (0, jnp.clip(s - 8, 0, 1))),
        ],
        out_specs=pl.BlockSpec((8, 1, BLOCK, SEQ_DEV), lambda s: (0, s % 2, s // 2, 0)),
        out_shape=jax.ShapeDtypeStruct((8, 2, 5 * BLOCK, SEQ_DEV), BF16),
        flops=2 * 128 * 4096 * 2048,
        bytes_accessed=19 * MIB,
        name="project",
    )(tokens, out_grad, weight, out_weight, filters)


def cosine_matrix():
    odd = 2 * np.arange(SEQ, dtype=np.int64) + 1
    turns = np.outer(odd, odd) % (8 * SEQ)
    return np.cos(turns * (2.0 * np.pi / (8 * SEQ))).astype(ml_dtypes.bfloat16)


def frequency_rows():
    half = (2 * np.arange(SEQ) + 1) * (np.pi / (4 * SEQ))
    sign = 1.0 - 2.0 * (np.arange(SEQ) % 2)
    rows = np.zeros((8, SEQ), np.float32)
    rows[0], rows[1], rows[2] = np.cos(half), np.sin(half), sign
    return rows


def convolve(received, matrix, rows, flip):
    chunk = 512
    n_chunks = SEQ // chunk

    def kernel(r_ref, m_hbm, w_ref, j_ref, b_ref, o_ref, m_ref, x_ref, y_ref, sem):
        copies = []
        for n in range(n_chunks):
            lanes = pl.ds(n * chunk, chunk)
            copies.append(pltpu.make_async_copy(m_hbm.at[:, lanes], m_ref.at[:, lanes], sem.at[n]))
            copies[-1].start()
        rev = j_ref[...]
        for b in range(16):
            part = r_ref[b]
            key, value = part[32:64].astype(F32), part[64:96].astype(F32)
            query, gate = part[0:32].astype(F32), part[96:128].astype(F32)
            lanes = pl.ds(b * 128, 128)
            x_ref[0:32, lanes] = part[128:160]
            x_ref[32:64, lanes] = (key * value).astype(BF16)
            x_ref[64:96, lanes] = (gate * query).astype(BF16)
        for b in range(8):
            x_ref[96:192, pl.ds((7 - b) * 256, 256)] = dot(x_ref[0:96, pl.ds(b * 256, 256)], rev).astype(BF16)
        for n in range(n_chunks):
            lanes = pl.ds(n * chunk, chunk)
            copies[n].wait()
            spec = dot(x_ref[...], m_ref[:, lanes])
            wr, wi, sign = w_ref[0:1, lanes], w_ref[1:2, lanes], w_ref[2:3, lanes]
            hr, mr, gr = spec[0:32], spec[32:64], spec[64:96]
            neg = -sign
            hi, mi, gi = spec[96:128] * neg, spec[128:160] * neg, spec[160:192] * neg
            hwr, hwi = hr * wr - hi * wi, hr * wi + hi * wr
            mwr, mwi = mr * wr - mi * wi, mr * wi + mi * wr
            y_ref[0:32, lanes] = (hwr * mr - hwi * mi).astype(BF16)
            y_ref[32:64, lanes] = (gr * hwr + gi * hwi).astype(BF16)
            y_ref[64:96, lanes] = (gr * mwr + gi * mwi).astype(BF16)
            imag = jnp.concatenate(
                [hwr * mi + hwi * mr, gi * hwr - gr * hwi, gi * mwr - gr * mwi], axis=0
            ).astype(BF16)
            for b in range(chunk // 256):
                at = SEQ - (n * chunk + (b + 1) * 256)
                y_ref[96:192, pl.ds(at, 256)] = dot(imag[:, b * 256 : (b + 1) * 256], rev).astype(BF16)
        scale = 1.0 / SEQ
        for n in range(n_chunks):
            lanes = pl.ds(n * chunk, chunk)
            back = dot(y_ref[...], m_ref[:, lanes])
            back = (back[0:96] - back[96:192] * w_ref[2:3, lanes]) * scale
            for b in range(chunk // 128):
                at = n * (chunk // 128) + b
                part = r_ref[at]
                cut = slice(b * 128, (b + 1) * 128)
                conv, mixed, raw = back[0:32, cut], back[32:64, cut], back[64:96, cut]
                query, key, value, gate = (part[32 * i : 32 * i + 32].astype(F32) for i in range(4))
                gq = (gate * conv).astype(BF16)
                gk = (mixed * value).astype(BF16)
                gv = (mixed * key).astype(BF16)
                pos = pl.ds(at * 128, 128)
                b_ref[0:32, pos] = gq
                b_ref[32:64, pos] = gk
                b_ref[64:96, pos] = gv
                b_ref[96:128, pos] = (query * conv).astype(BF16)
                o_ref[at, 0:32, :] = gq
                o_ref[at, 32:64, :] = gk
                o_ref[at, 64:96, :] = gv
                o_ref[at, 96:128, :] = (raw * (1.0 / math.sqrt(SEQ))).astype(BF16)

    vm = pl.BlockSpec(memory_space=pltpu.VMEM)
    return call(
        kernel,
        in_specs=[vm, pl.BlockSpec(memory_space=pl.ANY), vm, vm],
        out_specs=[vm, vm],
        out_shape=[
            jax.ShapeDtypeStruct((128, SEQ), BF16),
            jax.ShapeDtypeStruct((16, 128, 128), BF16),
        ],
        scratch_shapes=[
            pltpu.VMEM((SEQ, SEQ), BF16),
            pltpu.VMEM((192, SEQ), BF16),
            pltpu.VMEM((192, SEQ), BF16),
            pltpu.SemaphoreType.DMA((n_chunks,)),
        ],
        flops=4 * 192 * SEQ * SEQ,
        bytes_accessed=12 * MIB,
        name="convolve",
    )(received, matrix, rows, flip)


def input_partial(received, weight):
    def kernel(r_ref, w_ref, o_ref, f_ref, g_ref):
        @pl.when(pl.program_id(0) == 0)
        def _():
            for chip in range(8):
                for core in range(2):
                    at = core * 256 + chip * BLOCK
                    for j in range(3):
                        g_ref[j, at : at + BLOCK, :] = r_ref[2 * chip + core, j * BLOCK : (j + 1) * BLOCK, :]
            raw = [r_ref[2 * chip + core, 96:128, :] for core in range(2) for chip in range(8)]
            f_ref[...] = jnp.concatenate(raw, axis=0).astype(F32).T

        total = dot(w_ref[0], g_ref[0]) + dot(w_ref[1], g_ref[1]) + dot(w_ref[2], g_ref[2])
        o_ref[...] = total.astype(BF16).reshape(1, 512, SEQ_DEV)

    return call(
        kernel,
        grid=(8,),
        in_specs=[
            pl.BlockSpec((16, 128, 128), lambda s: (0, 0, 0)),
            pl.BlockSpec((3, 512, 512), lambda s: (0, s, 0)),
        ],
        out_specs=[
            pl.BlockSpec((1, 512, SEQ_DEV), lambda s: (s, 0, 0)),
            pl.BlockSpec((SEQ_DEV, 512), lambda s: (0, 0)),
        ],
        out_shape=[
            jax.ShapeDtypeStruct((8, 512, SEQ_DEV), BF16),
            jax.ShapeDtypeStruct((SEQ_DEV, 512), F32),
        ],
        scratch_shapes=[pltpu.VMEM((3, 512, SEQ_DEV), BF16)],
        flops=2 * 128 * 4096 * 1536,
        bytes_accessed=14 * MIB,
        name="input_partial",
    )(received, weight)


def sum_partials(parts):
    def kernel(p_ref, o_ref):
        total = p_ref[0].astype(F32)
        for i in range(1, 8):
            total = total + p_ref[i].astype(F32)
        o_ref[...] = total.T.astype(BF16)

    vm = pl.BlockSpec(memory_space=pltpu.VMEM)
    return call(
        kernel,
        in_specs=[vm],
        out_specs=vm,
        out_shape=jax.ShapeDtypeStruct((SEQ_DEV, 512), BF16),
        bytes_accessed=MIB,
        name="sum_partials",
    )(parts)


def turn_columns(received):
    def kernel(r_ref, o_ref):
        for b in range(4):
            for h in range(4):
                block = r_ref[b, h * 128 : (h + 1) * 128, :].astype(F32).T
                o_ref[h * 128 : (h + 1) * 128, b * 128 : (b + 1) * 128] = block.astype(BF16)

    return call(
        kernel,
        grid=(4,),
        in_specs=[pl.BlockSpec((4, 512, 128), lambda s: (s, 0, 0))],
        out_specs=pl.BlockSpec((512, 512), lambda s: (0, s)),
        out_shape=jax.ShapeDtypeStruct((512, SEQ), BF16),
        bytes_accessed=4 * MIB,
        name="turn_columns",
    )(received)


def weight_gradients(place, own_columns, other_columns, blocks):
    n_blocks = len(blocks)
    factor = 1.0 / math.sqrt(SEQ)

    def kernel(place_ref, own_ref, other_ref, *refs):
        block_refs = refs[:n_blocks]
        in_hbm, out_hbm, send_ref, g_ref, res_ref, sem, out_sem = refs[n_blocks:]
        core = place_ref[n_blocks]
        copies = [[], [], [], []]
        for j in range(4):
            for k in range(n_blocks):
                src = block_refs[k].at[pl.ds(j * BLOCK, BLOCK)]
                at = pl.multiple_of(place_ref[k] * BLOCK, BLOCK)
                copies[j].append(pltpu.make_async_copy(src, g_ref.at[j, pl.ds(at, BLOCK)], sem.at[j, k]))
                copies[j][-1].start()
        half = pl.multiple_of(core * 256, 256)
        outs = []
        for j in range(4):
            for copy in copies[j]:
                copy.wait()
            g = g_ref[j]
            if j < 3:
                send_ref[j * 256 : (j + 1) * 256, :] = (dot(other_ref[0:256], g, NT) * factor).astype(BF16)
                res_ref[j] = dot(own_ref[0:256], g, NT) * factor
                dst = in_hbm.at[j, :, pl.ds(half, 256)]
            else:
                send_ref[768:1024, :] = (dot(g, other_ref[256:512], NT) * factor).astype(BF16)
                res_ref[j] = dot(g, own_ref[256:512], NT) * factor
                dst = out_hbm.at[pl.ds(half, 256)]
            outs.append(pltpu.make_async_copy(res_ref.at[j], dst, out_sem.at[j]))
            outs[-1].start()
        for copy in outs:
            copy.wait()

    vm = pl.BlockSpec(memory_space=pltpu.VMEM)
    hbm = pl.BlockSpec(memory_space=pl.ANY)
    return call(
        kernel,
        in_specs=[pl.BlockSpec(memory_space=pltpu.SMEM), vm, vm] + [hbm] * n_blocks,
        out_specs=[hbm, hbm, vm],
        out_shape=[
            jax.ShapeDtypeStruct((3, 256, 512), F32),
            jax.ShapeDtypeStruct((512, 256), F32),
            jax.ShapeDtypeStruct((1024, 256), BF16),
        ],
        scratch_shapes=[
            pltpu.VMEM((4, 256, SEQ), BF16),
            pltpu.VMEM((4, 256, 256), F32),
            pltpu.SemaphoreType.DMA((4, n_blocks)),
            pltpu.SemaphoreType.DMA((4,)),
        ],
        flops=4 * 1024 * 256 * SEQ,
        bytes_accessed=10 * MIB,
        name="weight_gradients",
    )(place, own_columns, other_columns, *blocks)


def fill_halves(place, sent, in_grad, out_grad):
    def kernel(place_ref, s_ref, in_old, out_old, in_hbm, out_hbm, res_ref, sem):
        half = pl.multiple_of((1 - place_ref[8]) * 256, 256)
        outs = []
        for j in range(4):
            res_ref[j] = s_ref[j * 256 : (j + 1) * 256, :].astype(F32)
            dst = in_hbm.at[j, :, pl.ds(half, 256)] if j < 3 else out_hbm.at[pl.ds(half, 256)]
            outs.append(pltpu.make_async_copy(res_ref.at[j], dst, sem.at[j]))
            outs[-1].start()
        for copy in outs:
            copy.wait()

    vm = pl.BlockSpec(memory_space=pltpu.VMEM)
    hbm = pl.BlockSpec(memory_space=pl.ANY)
    return call(
        kernel,
        in_specs=[pl.BlockSpec(memory_space=pltpu.SMEM), vm, hbm, hbm],
        out_specs=[hbm, hbm],
        out_shape=[jax.ShapeDtypeStruct((3, 256, 512), F32), jax.ShapeDtypeStruct((512, 256), F32)],
        scratch_shapes=[pltpu.VMEM((4, 256, 256), F32), pltpu.SemaphoreType.DMA((4,))],
        input_output_aliases={2: 0, 3: 1},
        bytes_accessed=3 * MIB,
        name="fill_halves",
    )(place, sent, in_grad, out_grad)


def chip_hop(x_flip, z_step):
    pairs = []
    for i in range(16):
        x, z, core = i // 8, i // 2 % 4, i % 2
        pairs.append((i, ((x ^ x_flip) * 4 + (z + z_step) % 4) * 2 + core))
    return pairs


def swap_cores(value):
    return lax.ppermute(value, "ctx", [(i, i ^ 1) for i in range(16)])


def swap(pieces, axis):
    return lax.all_to_all(pieces, axis, 0, 0, tiled=True)


def on_device(tokens, out_grad, in_weight, out_weight, filters):
    position = lax.axis_index("ctx")
    chip, core = position // 2, position % 2
    weight = jnp.transpose(in_weight, (1, 0, 2))
    columns = swap(split_columns(tokens, out_grad), "ctx")
    signals = project(tokens, out_grad, weight, out_weight, filters)
    signals = swap(signals.reshape(16, 5 * BLOCK, SEQ_DEV), "ctx")
    columns = turn_columns(columns)
    other_columns = swap_cores(columns)
    flip = jnp.asarray(np.eye(256)[::-1].astype(ml_dtypes.bfloat16))
    block, pieces = convolve(
        signals, jnp.asarray(cosine_matrix()), jnp.asarray(frequency_rows()), flip
    )
    pieces = swap(pieces, "ctx")
    blocks, sources = [block], [chip]
    for x_flip, z_step in ((0, 1), (0, 3), (1, 0), (1, 1), (1, 3), (0, 2), (1, 2)):
        blocks.append(lax.ppermute(block, "ctx", chip_hop(x_flip, z_step)))
        sources.append((chip // 4 ^ x_flip) * 4 + (chip % 4 - z_step) % 4)
    place = jnp.stack(sources + [core]).astype(jnp.int32)
    partial, filter_grad = input_partial(pieces, weight)
    input_grad = sum_partials(swap(partial, "mp"))
    in_grad, out_weight_grad, send = weight_gradients(place, columns, other_columns, blocks)
    in_grad, out_weight_grad = fill_halves(place, swap_cores(send), in_grad, out_weight_grad)
    return (input_grad, jnp.transpose(in_grad, (1, 0, 2)), out_weight_grad, filter_grad)


def solution(mesh):
    in_specs = (P("ctx", None), P("ctx", None), P(None, None, "mp"), P("mp", None), P("ctx", "mp"))
    out_specs = (P("ctx", "mp"), P("ctx", None, "mp"), P("mp", "ctx"), P("ctx", "mp"))
    return jax.shard_map(
        on_device, mesh=mesh, in_specs=in_specs, out_specs=out_specs, check_vma=False
    )
```

```python
import math

import jax
import jax.numpy as jnp
import ml_dtypes
import numpy as np
from jax import lax
from jax.experimental import pallas as pl
from jax.experimental.pallas import tpu as pltpu
from jax.sharding import PartitionSpec as P

F32 = jnp.float32
BF16 = jnp.bfloat16
NT = (((1,), (1,)), ((), ()))
NN = (((1,), (0,)), ((), ()))
MIB = 1 << 20
BLOCK = 32
SEQ_DEV = 128
SEQ = 2048


def dot(a, b, dims=NN):
    return lax.dot_general(a, b, dims, preferred_element_type=F32)


def in_hbm(value):
    return pltpu.with_memory_space_constraint(value, pltpu.HBM)


def in_vmem(value):
    return pltpu.with_memory_space_constraint(value, pltpu.VMEM)


class Stream:
    def __init__(self, groups, ahead):
        self.groups, self.started, self.ahead = groups, 0, ahead
        self.start(ahead)

    def start(self, upto):
        while self.started < min(upto, len(self.groups)):
            for copy in self.groups[self.started]:
                copy.start()
            self.started += 1

    def wait(self, index):
        for copy in self.groups[index]:
            copy.wait()
        self.start(index + 1 + self.ahead)


def call(kernel, *, flops=0, bytes_accessed=0, vmem=32, **kw):
    return pl.pallas_call(
        kernel,
        compiler_params=pltpu.CompilerParams(vmem_limit_bytes=vmem * MIB),
        cost_estimate=pl.CostEstimate(flops=flops, bytes_accessed=bytes_accessed, transcendentals=0),
        **kw,
    )


def split_columns(quarter, tokens, out_grad):
    def kernel(y_ref, t_hbm, g_hbm, o_ref, sem):
        copies = []
        for chip in range(8):
            lanes = pl.ds(pl.multiple_of(chip * 512 + y_ref[0] * 128, 128), 128)
            copies.append(pltpu.make_async_copy(t_hbm.at[:, lanes], o_ref.at[chip, 0], sem.at[chip, 0]))
            copies.append(pltpu.make_async_copy(g_hbm.at[:, lanes], o_ref.at[chip, 1], sem.at[chip, 1]))
        for copy in copies:
            copy.start()
        for copy in copies:
            copy.wait()

    hbm = pl.BlockSpec(memory_space=pl.ANY)
    return call(
        kernel,
        in_specs=[pl.BlockSpec(memory_space=pltpu.SMEM), hbm, hbm],
        out_specs=pl.BlockSpec(memory_space=pltpu.VMEM),
        out_shape=jax.ShapeDtypeStruct((8, 2, SEQ_DEV, 128), BF16),
        scratch_shapes=[pltpu.SemaphoreType.DMA((8, 2))],
        bytes_accessed=MIB,
        vmem=4,
        name="split_columns",
    )(quarter, in_hbm(tokens), in_hbm(out_grad))


def project(tokens, out_grad, weight, out_weight, filters):
    depth = 2048
    steps = 4096 // depth
    gate = 256

    def kernel(t_hbm, g_hbm, f_hbm, w_hbm, ow_hbm, o_ref, f_ref, t_ref, g_ref, w_ref, ow_ref, sem):
        def fetch(src, dst, at):
            return pltpu.make_async_copy(src, dst, sem.at[at])

        gates = [pl.ds(gate * i, gate) for i in range(512 // gate)]
        groups = [[fetch(ow_hbm.at[rows], ow_ref.at[rows], i)] for i, rows in enumerate(gates)]
        first = len(groups)
        groups[0] = [fetch(f_hbm, f_ref, first), fetch(g_hbm, g_ref, first + 1)] + groups[0]
        for j in range(3):
            for k in range(steps):
                rows = pl.ds(k * depth, depth)
                at = first + 3 + j * steps + k
                groups.append([fetch(w_hbm.at[j, rows], w_ref.at[j, rows], at)])
        groups[first].append(fetch(t_hbm, t_ref, first + 2))
        stream = Stream(groups, 8)

        def put(first, sig, rows):
            n = rows.shape[0] // BLOCK
            core, chip = first // 256, first % 256 // BLOCK
            o_ref[chip : chip + n, core, sig * BLOCK : (sig + 1) * BLOCK, :] = rows.astype(BF16).reshape(
                n, BLOCK, SEQ_DEV
            )

        for i in range(512 // gate):
            stream.wait(i)
            put(i * gate, 3, dot(ow_ref[i * gate : (i + 1) * gate], g_ref[...], NT))
        for c in range(2):
            put(c * 256, 4, f_ref[:, c * 256 : (c + 1) * 256].T)
        for j in range(3):
            total = None
            for k in range(steps):
                stream.wait(first + j * steps + k)
                part = dot(t_ref[:, k * depth : (k + 1) * depth], w_ref[j, k * depth : (k + 1) * depth])
                total = part if total is None else total + part
            for c in range(2):
                put(c * 256, j, total[:, c * 256 : (c + 1) * 256].T)

    vm = pl.BlockSpec(memory_space=pltpu.VMEM)
    hbm = pl.BlockSpec(memory_space=pl.ANY)
    return call(
        kernel,
        in_specs=[hbm] * 5,
        out_specs=vm,
        out_shape=jax.ShapeDtypeStruct((8, 2, 5 * BLOCK, SEQ_DEV), BF16),
        scratch_shapes=[
            pltpu.VMEM((SEQ_DEV, 512), F32),
            pltpu.VMEM((SEQ_DEV, 4096), BF16),
            pltpu.VMEM((SEQ_DEV, 4096), BF16),
            pltpu.VMEM((3, 4096, 512), BF16),
            pltpu.VMEM((512, 4096), BF16),
            pltpu.SemaphoreType.DMA((3 + 512 // gate + 3 * steps,)),
        ],
        flops=2 * 128 * 4096 * 2048,
        bytes_accessed=19 * MIB,
        vmem=28,
        name="project",
    )(in_hbm(tokens), in_hbm(out_grad), in_hbm(filters), in_hbm(weight), in_hbm(out_weight))


def cosine_matrix():
    odd = 2 * np.arange(SEQ, dtype=np.int64) + 1
    turns = np.outer(odd, odd) % (8 * SEQ)
    return np.cos(turns * (2.0 * np.pi / (8 * SEQ))).astype(ml_dtypes.bfloat16)


def frequency_rows():
    half = (2 * np.arange(SEQ) + 1) * (np.pi / (4 * SEQ))
    sign = 1.0 - 2.0 * (np.arange(SEQ) % 2)
    rows = np.zeros((8, SEQ), np.float32)
    rows[0], rows[1], rows[2] = np.cos(half), np.sin(half), sign
    return rows


def convolve(received, matrix, rows, flip):
    chunk = 512
    n_chunks = SEQ // chunk

    def kernel(r_ref, m_hbm, w_ref, j_ref, b_ref, o_ref, m_ref, x_ref, y_ref, sem):
        chunks = [pl.ds(n * chunk, chunk) for n in range(n_chunks)]
        stream = Stream(
            [[pltpu.make_async_copy(m_hbm.at[:, c], m_ref.at[:, c], sem.at[n])] for n, c in enumerate(chunks)], 4
        )
        rev = j_ref[...]
        for b in range(16):
            part = r_ref[b]
            key, value = part[32:64].astype(F32), part[64:96].astype(F32)
            query, gate = part[0:32].astype(F32), part[96:128].astype(F32)
            lanes = pl.ds(b * 128, 128)
            x_ref[0:32, lanes] = part[128:160]
            x_ref[32:64, lanes] = (key * value).astype(BF16)
            x_ref[64:96, lanes] = (gate * query).astype(BF16)
        for b in range(8):
            x_ref[96:192, pl.ds((7 - b) * 256, 256)] = dot(x_ref[0:96, pl.ds(b * 256, 256)], rev).astype(BF16)
        for n in range(n_chunks):
            lanes = pl.ds(n * chunk, chunk)
            stream.wait(n)
            spec = dot(x_ref[...], m_ref[:, lanes])
            wr, wi, sign = w_ref[0:1, lanes], w_ref[1:2, lanes], w_ref[2:3, lanes]
            hr, mr, gr = spec[0:32], spec[32:64], spec[64:96]
            neg = -sign
            hi, mi, gi = spec[96:128] * neg, spec[128:160] * neg, spec[160:192] * neg
            hwr, hwi = hr * wr - hi * wi, hr * wi + hi * wr
            mwr, mwi = mr * wr - mi * wi, mr * wi + mi * wr
            y_ref[0:32, lanes] = (hwr * mr - hwi * mi).astype(BF16)
            y_ref[32:64, lanes] = (gr * hwr + gi * hwi).astype(BF16)
            y_ref[64:96, lanes] = (gr * mwr + gi * mwi).astype(BF16)
            imag = jnp.concatenate(
                [hwr * mi + hwi * mr, gi * hwr - gr * hwi, gi * mwr - gr * mwi], axis=0
            ).astype(BF16)
            for b in range(chunk // 256):
                at = SEQ - (n * chunk + (b + 1) * 256)
                y_ref[96:192, pl.ds(at, 256)] = dot(imag[:, b * 256 : (b + 1) * 256], rev).astype(BF16)
        scale = 1.0 / SEQ
        for n in range(n_chunks):
            lanes = pl.ds(n * chunk, chunk)
            back = dot(y_ref[...], m_ref[:, lanes])
            back = (back[0:96] - back[96:192] * w_ref[2:3, lanes]) * scale
            for b in range(chunk // 128):
                at = n * (chunk // 128) + b
                part = r_ref[at]
                cut = slice(b * 128, (b + 1) * 128)
                conv, mixed, raw = back[0:32, cut], back[32:64, cut], back[64:96, cut]
                query, key, value, gate = (part[32 * i : 32 * i + 32].astype(F32) for i in range(4))
                gq = (gate * conv).astype(BF16)
                gk = (mixed * value).astype(BF16)
                gv = (mixed * key).astype(BF16)
                pos = pl.ds((at % 2 * 8 + at // 2) * 128, 128)
                b_ref[0:32, pos] = gq
                b_ref[32:64, pos] = gk
                b_ref[64:96, pos] = gv
                b_ref[96:128, pos] = (query * conv).astype(BF16)
                o_ref[at, 0:32, :] = gq
                o_ref[at, 32:64, :] = gk
                o_ref[at, 64:96, :] = gv
                o_ref[at, 96:128, :] = (raw * (1.0 / math.sqrt(SEQ))).astype(BF16)

    vm = pl.BlockSpec(memory_space=pltpu.VMEM)
    return call(
        kernel,
        in_specs=[vm, pl.BlockSpec(memory_space=pl.ANY), vm, vm],
        out_specs=[vm, vm],
        out_shape=[
            jax.ShapeDtypeStruct((128, SEQ), BF16),
            jax.ShapeDtypeStruct((16, 128, 128), BF16),
        ],
        scratch_shapes=[
            pltpu.VMEM((SEQ, SEQ), BF16),
            pltpu.VMEM((192, SEQ), BF16),
            pltpu.VMEM((192, SEQ), BF16),
            pltpu.SemaphoreType.DMA((n_chunks,)),
        ],
        flops=4 * 192 * SEQ * SEQ,
        bytes_accessed=12 * MIB,
        vmem=20,
        name="convolve",
    )(received, in_hbm(matrix), rows, flip)


def input_partial(received, weight):
    steps = 8
    depth = 4096 // steps

    def kernel(r_ref, w_hbm, o_ref, f_ref, w_ref, g_ref, sem):
        groups = []
        for s in range(steps):
            rows = pl.ds(s * depth, depth)
            groups.append(
                [
                    pltpu.make_async_copy(w_hbm.at[j, rows], w_ref.at[rows, pl.ds(j * 512, 512)], sem.at[s, j])
                    for j in range(3)
                ]
            )
        stream = Stream(groups, steps)
        for chip in range(8):
            for core in range(2):
                at = core * 256 + chip * BLOCK
                for j in range(4):
                    g_ref[j * 512 + at : j * 512 + at + BLOCK, :] = r_ref[
                        2 * chip + core, j * BLOCK : (j + 1) * BLOCK, :
                    ]
        grads = g_ref[0:1536].astype(F32).T.astype(BF16)
        f_ref[...] = g_ref[1536:2048].astype(F32).T
        for s in range(steps):
            stream.wait(s)
            o_ref[s] = dot(grads, w_ref[s * depth : (s + 1) * depth], NT).astype(BF16)

    vm = pl.BlockSpec(memory_space=pltpu.VMEM)
    return call(
        kernel,
        in_specs=[vm, pl.BlockSpec(memory_space=pl.ANY)],
        out_specs=[vm, vm],
        out_shape=[
            jax.ShapeDtypeStruct((8, SEQ_DEV, 512), BF16),
            jax.ShapeDtypeStruct((SEQ_DEV, 512), F32),
        ],
        scratch_shapes=[
            pltpu.VMEM((4096, 1536), BF16),
            pltpu.VMEM((2048, SEQ_DEV), BF16),
            pltpu.SemaphoreType.DMA((steps, 3)),
        ],
        flops=2 * 128 * 4096 * 1536,
        bytes_accessed=14 * MIB,
        vmem=24,
        name="input_partial",
    )(received, in_hbm(weight))


def sum_partials(parts):
    def kernel(p_ref, o_ref):
        total = p_ref[0].astype(F32)
        for i in range(1, 8):
            total = total + p_ref[i].astype(F32)
        o_ref[...] = total.astype(BF16)

    vm = pl.BlockSpec(memory_space=pltpu.VMEM)
    return call(
        kernel,
        in_specs=[vm],
        out_specs=vm,
        out_shape=jax.ShapeDtypeStruct((SEQ_DEV, 512), BF16),
        bytes_accessed=MIB,
        name="sum_partials",
    )(parts)


def pair(first, second, third, fourth):
    def kernel(a, b, c, d, o_ref, p_ref, sem):
        copies = []
        for i, (src, out) in enumerate(((a, o_ref), (b, o_ref), (c, p_ref), (d, p_ref))):
            copies.append(pltpu.make_async_copy(src, out.at[pl.ds(i % 2 * 128, 128)], sem.at[i]))
        for copy in copies:
            copy.start()
        for copy in copies:
            copy.wait()

    hbm = pl.BlockSpec(memory_space=pl.ANY)
    return call(
        kernel,
        in_specs=[hbm] * 4,
        out_specs=[pl.BlockSpec(memory_space=pltpu.VMEM)] * 2,
        out_shape=[jax.ShapeDtypeStruct((256, SEQ), BF16)] * 2,
        scratch_shapes=[pltpu.SemaphoreType.DMA((4,))],
        bytes_accessed=4 * MIB,
        vmem=8,
        name="pair",
    )(in_hbm(first), in_hbm(second), in_hbm(third), in_hbm(fourth))


def weight_gradients(place, columns, blocks):
    factor = 1.0 / math.sqrt(SEQ)
    first_rows = [first for _, first in blocks]

    def kernel(place_ref, *refs):
        column_refs, block_refs = refs[:8], refs[8:16]
        in_hbm, out_hbm, send_ref, t_ref, g_ref, res_ref, t_sem, sem, out_sem = refs[16:]
        core = place_ref[8]
        t_copies = [[], []]
        for j in range(2):
            for i in range(8):
                lanes = pl.ds(pl.multiple_of(place_ref[9 + i % 4] * 128, 128), 128)
                t_copies[j].append(
                    pltpu.make_async_copy(
                        column_refs[i].at[:, j], t_ref.at[j, i // 4, :, :, lanes], t_sem.at[j, i]
                    )
                )
        copies = [[], [], [], []]
        for j in range(4):
            for k in range(8):
                at = pl.multiple_of(place_ref[k] * BLOCK, BLOCK)
                copies[j].append(
                    pltpu.make_async_copy(
                        block_refs[k].at[pl.ds(first_rows[k] + j * BLOCK, BLOCK)], g_ref.at[j, pl.ds(at, BLOCK)], sem.at[j, k]
                    )
                )
        for copy in t_copies[0] + copies[0] + copies[1] + copies[2] + t_copies[1] + copies[3]:
            copy.start()
        half = pl.multiple_of(core * 256, 256)
        rest = pl.multiple_of((1 - core) * 256, 256)
        outs = []
        for j in range(4):
            for copy in copies[j] + (t_copies[j // 3] if j % 3 == 0 else []):
                copy.wait()
            own = g_ref[j, :, pl.ds(pl.multiple_of(core * 1024, 1024), 1024)]
            other = g_ref[j, :, pl.ds(pl.multiple_of((1 - core) * 1024, 1024), 1024)]
            total = dot(own, t_ref[j // 3, 0].reshape(1024, 512)) + dot(other, t_ref[j // 3, 1].reshape(1024, 512))
            total = total * factor
            if j < 3:
                res_ref[j] = total.T
                send_ref[j * 256 : (j + 1) * 256, :] = res_ref[j, pl.ds(rest, 256), :].astype(BF16)
                src, dst = res_ref.at[j, pl.ds(half, 256)], in_hbm.at[j, :, pl.ds(half, 256)]
            else:
                res_ref[3, 0:256] = total[:, 0:256]
                res_ref[3, 256:512] = total[:, 256:512]
                send_ref[768:1024, :] = res_ref[3, pl.ds(rest, 256), :].astype(BF16)
                src, dst = res_ref.at[3, pl.ds(half, 256)], out_hbm.at[pl.ds(half, 256)]
            outs.append(pltpu.make_async_copy(src, dst, out_sem.at[j]))
            outs[-1].start()
        for copy in outs:
            copy.wait()

    vm = pl.BlockSpec(memory_space=pltpu.VMEM)
    hbm = pl.BlockSpec(memory_space=pl.ANY)
    return call(
        kernel,
        in_specs=[pl.BlockSpec(memory_space=pltpu.SMEM)] + [hbm] * 16,
        out_specs=[hbm, hbm, vm],
        out_shape=[
            jax.ShapeDtypeStruct((3, 256, 512), F32),
            jax.ShapeDtypeStruct((512, 256), F32),
            jax.ShapeDtypeStruct((1024, 256), BF16),
        ],
        scratch_shapes=[
            pltpu.VMEM((2, 2, 8, SEQ_DEV, 512), BF16),
            pltpu.VMEM((4, 256, SEQ), BF16),
            pltpu.VMEM((4, 512, 256), F32),
            pltpu.SemaphoreType.DMA((2, 8)),
            pltpu.SemaphoreType.DMA((4, 8)),
            pltpu.SemaphoreType.DMA((4,)),
        ],
        flops=4 * 1024 * 256 * SEQ,
        bytes_accessed=10 * MIB,
        vmem=24,
        name="weight_gradients",
    )(place, *[in_hbm(value) for value in columns + [block for block, _ in blocks]])


def fill_halves(place, sent, in_grad, out_grad):
    def kernel(place_ref, s_ref, in_old, out_old, in_hbm, out_hbm, res_ref, sem):
        half = pl.multiple_of((1 - place_ref[8]) * 256, 256)
        outs = []
        for j in range(4):
            res_ref[j] = s_ref[j * 256 : (j + 1) * 256, :].astype(F32)
            dst = in_hbm.at[j, :, pl.ds(half, 256)] if j < 3 else out_hbm.at[pl.ds(half, 256)]
            outs.append(pltpu.make_async_copy(res_ref.at[j], dst, sem.at[j]))
            outs[-1].start()
        for copy in outs:
            copy.wait()

    vm = pl.BlockSpec(memory_space=pltpu.VMEM)
    hbm = pl.BlockSpec(memory_space=pl.ANY)
    return call(
        kernel,
        in_specs=[pl.BlockSpec(memory_space=pltpu.SMEM), vm, hbm, hbm],
        out_specs=[hbm, hbm],
        out_shape=[jax.ShapeDtypeStruct((3, 256, 512), F32), jax.ShapeDtypeStruct((512, 256), F32)],
        scratch_shapes=[pltpu.VMEM((4, 256, 256), F32), pltpu.SemaphoreType.DMA((4,))],
        input_output_aliases={2: 0, 3: 1},
        bytes_accessed=3 * MIB,
        vmem=8,
        name="fill_halves",
    )(place, sent, in_hbm(in_grad), in_hbm(out_grad))


def chip_hop(x_flip, z_step):
    pairs = []
    for i in range(16):
        x, z, core = i // 8, i // 2 % 4, i % 2
        pairs.append((i, ((x ^ x_flip) * 4 + (z + z_step) % 4) * 2 + core))
    return pairs


def swap_cores(value):
    return lax.ppermute(value, "ctx", [(i, i ^ 1) for i in range(16)])


def swap(pieces, axis, groups=None):
    return lax.all_to_all(pieces, axis, 0, 0, axis_index_groups=groups, tiled=True)


HOPS = ((0, 0), (0, 1), (0, 3), (1, 0), (0, 2), (1, 1), (1, 3), (1, 2))


def hop(value, x_flip, z_step):
    return lax.ppermute(value, "ctx", chip_hop(x_flip, z_step))


def after(value, *others):
    return lax.optimization_barrier((value,) + others)[0]


def hop_y(value, step):
    return lax.ppermute(value, "mp", [(i, i // 4 * 4 + (i % 4 + step) % 4) for i in range(8)])


def on_device(tokens, out_grad, in_weight, out_weight, filters):
    position = lax.axis_index("ctx")
    core, x, z = position & 1, position >> 3, (position >> 1) & 3
    y = lax.axis_index("mp") & 3
    place = [((x ^ f) << 2) + ((z - s) & 3) for f, s in HOPS] + [core] + [(y - s) & 3 for s in range(4)]
    place = jnp.stack(place).astype(jnp.int32)
    weight = jnp.transpose(in_weight, (1, 0, 2))
    columns = split_columns(y.astype(jnp.int32)[None], tokens, out_grad)
    signals = project(after(tokens, columns), out_grad, weight, out_weight, filters)
    columns = swap(columns, "ctx", [list(range(c, 16, 2)) for c in range(2)])
    signals, columns = lax.optimization_barrier((signals, columns))
    signals = swap(signals.reshape(16, 5 * BLOCK, SEQ_DEV), "ctx")
    columns = [columns] + [hop_y(columns, s) for s in (1, 2, 3)]
    flip = jnp.asarray(np.eye(256)[::-1].astype(ml_dtypes.bfloat16))
    block, pieces = convolve(
        signals, jnp.asarray(cosine_matrix()), jnp.asarray(frequency_rows()), flip
    )
    up, down, flipped = hop(block, 0, 1), hop(block, 0, 3), hop(block, 1, 0)
    pieces = swap(pieces, "ctx")
    up, down, flipped, pieces, *columns = lax.optimization_barrier((up, down, flipped, pieces, *columns))
    across, two = pair(up, down, block, flipped)
    across, two = hop(across, 1, 0), hop(two, 0, 2)
    partial, filter_grad = input_partial(pieces, weight)
    parts = swap(partial, "mp")
    parts, across, two = lax.optimization_barrier((parts, across, two))
    columns += [swap_cores(value) for value in columns]
    input_grad = sum_partials(parts)
    blocks = [(block, 0), (up, 0), (down, 0), (flipped, 0), (two, 0), (across, 0), (across, 128), (two, 128)]
    in_grad, out_weight_grad, send = weight_gradients(after(place, input_grad), columns, blocks)
    in_grad, out_weight_grad = fill_halves(place, swap_cores(send), in_grad, out_weight_grad)
    return (input_grad, jnp.transpose(in_grad, (1, 0, 2)), out_weight_grad, filter_grad)


def solution(mesh):
    in_specs = (P("ctx", None), P("ctx", None), P(None, None, "mp"), P("mp", None), P("ctx", "mp"))
    out_specs = (P("ctx", "mp"), P("ctx", None, "mp"), P("mp", "ctx"), P("ctx", "mp"))
    return jax.shard_map(
        on_device, mesh=mesh, in_specs=in_specs, out_specs=out_specs, check_vma=False
    )
```

```python
import math

import jax
import jax.numpy as jnp
import ml_dtypes
import numpy as np
from jax import lax
from jax.experimental import pallas as pl
from jax.experimental.pallas import tpu as pltpu
from jax.sharding import PartitionSpec as P

F32 = jnp.float32
BF16 = jnp.bfloat16
NT = (((1,), (1,)), ((), ()))
NN = (((1,), (0,)), ((), ()))
MIB = 1 << 20
BLOCK = 32
SEQ_DEV = 128
SEQ = 2048


def dot(a, b, dims=NN):
    return lax.dot_general(a, b, dims, preferred_element_type=F32)


def in_hbm(value):
    return pltpu.with_memory_space_constraint(value, pltpu.HBM)


def in_vmem(value):
    return pltpu.with_memory_space_constraint(value, pltpu.VMEM)


class Stream:
    def __init__(self, groups, ahead):
        self.groups, self.started, self.ahead = groups, 0, ahead
        self.start(ahead)

    def start(self, upto):
        while self.started < min(upto, len(self.groups)):
            for copy in self.groups[self.started]:
                copy.start()
            self.started += 1

    def wait(self, index):
        for copy in self.groups[index]:
            copy.wait()
        self.start(index + 1 + self.ahead)


def call(kernel, *, flops=0, bytes_accessed=0, vmem=32, **kw):
    return pl.pallas_call(
        kernel,
        compiler_params=pltpu.CompilerParams(vmem_limit_bytes=vmem * MIB),
        cost_estimate=pl.CostEstimate(flops=flops, bytes_accessed=bytes_accessed, transcendentals=0),
        **kw,
    )


def project(quarter, tokens, out_grad, weight, out_weight, filters):
    depth = 2048
    steps = 4096 // depth
    gate = 256

    def kernel(y_ref, t_hbm, g_hbm, f_hbm, w_hbm, ow_hbm, o_ref, f_ref, t_ref, g_ref, w_ref, ow_ref, sem):
        def fetch(src, dst, at):
            return pltpu.make_async_copy(src, dst, sem.at[at])

        gates = [pl.ds(gate * i, gate) for i in range(512 // gate)]
        groups = [[fetch(ow_hbm.at[rows], ow_ref.at[rows], i)] for i, rows in enumerate(gates)]
        first = len(groups)
        groups[0] = [fetch(f_hbm, f_ref, first), fetch(g_hbm, g_ref, first + 1)] + groups[0]
        for j in range(3):
            for k in range(steps):
                rows = pl.ds(k * depth, depth)
                at = first + 3 + j * steps + k
                groups.append([fetch(w_hbm.at[j, rows], w_ref.at[j, rows], at)])
        groups[first].append(fetch(t_hbm, t_ref, first + 2))
        stream = Stream(groups, 8)

        def put(first, sig, rows):
            n = rows.shape[0] // BLOCK
            core, chip = first // 256, first % 256 // BLOCK
            o_ref[chip : chip + n, core, sig * BLOCK : (sig + 1) * BLOCK, :] = rows.astype(BF16).reshape(
                n, BLOCK, SEQ_DEV
            )

        for i in range(512 // gate):
            stream.wait(i)
            put(i * gate, 3, dot(ow_ref[i * gate : (i + 1) * gate], g_ref[...], NT))
        for c in range(2):
            put(c * 256, 4, f_ref[:, c * 256 : (c + 1) * 256].T)
        for chip in range(8):
            lanes = pl.ds(pl.multiple_of(chip * 512 + y_ref[0] * 128, 128), 128)
            o_ref[chip, 1, 5 * BLOCK :, :] = g_ref[:, lanes]
        for j in range(3):
            total = None
            for k in range(steps):
                stream.wait(first + j * steps + k)
                part = dot(t_ref[:, k * depth : (k + 1) * depth], w_ref[j, k * depth : (k + 1) * depth])
                total = part if total is None else total + part
            if j == 0:
                for chip in range(8):
                    lanes = pl.ds(pl.multiple_of(chip * 512 + y_ref[0] * 128, 128), 128)
                    o_ref[chip, 0, 5 * BLOCK :, :] = t_ref[:, lanes]
            for c in range(2):
                put(c * 256, j, total[:, c * 256 : (c + 1) * 256].T)

    vm = pl.BlockSpec(memory_space=pltpu.VMEM)
    hbm = pl.BlockSpec(memory_space=pl.ANY)
    return call(
        kernel,
        in_specs=[pl.BlockSpec(memory_space=pltpu.SMEM)] + [hbm] * 5,
        out_specs=vm,
        out_shape=jax.ShapeDtypeStruct((8, 2, 5 * BLOCK + 128, SEQ_DEV), BF16),
        scratch_shapes=[
            pltpu.VMEM((SEQ_DEV, 512), F32),
            pltpu.VMEM((SEQ_DEV, 4096), BF16),
            pltpu.VMEM((SEQ_DEV, 4096), BF16),
            pltpu.VMEM((3, 4096, 512), BF16),
            pltpu.VMEM((512, 4096), BF16),
            pltpu.SemaphoreType.DMA((3 + 512 // gate + 3 * steps,)),
        ],
        flops=2 * 128 * 4096 * 2048,
        bytes_accessed=19 * MIB,
        vmem=28,
        name="project",
    )(quarter, in_hbm(tokens), in_hbm(out_grad), in_hbm(filters), in_hbm(weight), in_hbm(out_weight))


def cosine_matrix():
    odd = 2 * np.arange(SEQ, dtype=np.int64) + 1
    turns = np.outer(odd, odd) % (8 * SEQ)
    return np.cos(turns * (2.0 * np.pi / (8 * SEQ))).astype(ml_dtypes.bfloat16)


def frequency_rows():
    half = (2 * np.arange(SEQ) + 1) * (np.pi / (4 * SEQ))
    sign = 1.0 - 2.0 * (np.arange(SEQ) % 2)
    rows = np.zeros((8, SEQ), np.float32)
    rows[0], rows[1], rows[2] = np.cos(half), np.sin(half), sign
    return rows


def convolve(received, matrix, rows, flip):
    chunk = 512
    n_chunks = SEQ // chunk

    def kernel(r_ref, m_hbm, w_ref, j_ref, b_ref, o_ref, c_ref, m_ref, x_ref, y_ref, sem):
        chunks = [pl.ds(n * chunk, chunk) for n in range(n_chunks)]
        stream = Stream(
            [[pltpu.make_async_copy(m_hbm.at[:, c], m_ref.at[:, c], sem.at[n])] for n, c in enumerate(chunks)], 4
        )
        rev = j_ref[...]
        c_ref[...] = r_ref[:, 5 * BLOCK :, :]
        for b in range(16):
            part = r_ref[b]
            key, value = part[32:64].astype(F32), part[64:96].astype(F32)
            query, gate = part[0:32].astype(F32), part[96:128].astype(F32)
            lanes = pl.ds(b * 128, 128)
            x_ref[0:32, lanes] = part[128:160]
            x_ref[32:64, lanes] = (key * value).astype(BF16)
            x_ref[64:96, lanes] = (gate * query).astype(BF16)
        for b in range(8):
            x_ref[96:192, pl.ds((7 - b) * 256, 256)] = dot(x_ref[0:96, pl.ds(b * 256, 256)], rev).astype(BF16)
        for n in range(n_chunks):
            lanes = pl.ds(n * chunk, chunk)
            stream.wait(n)
            spec = dot(x_ref[...], m_ref[:, lanes])
            wr, wi, sign = w_ref[0:1, lanes], w_ref[1:2, lanes], w_ref[2:3, lanes]
            hr, mr, gr = spec[0:32], spec[32:64], spec[64:96]
            neg = -sign
            hi, mi, gi = spec[96:128] * neg, spec[128:160] * neg, spec[160:192] * neg
            hwr, hwi = hr * wr - hi * wi, hr * wi + hi * wr
            mwr, mwi = mr * wr - mi * wi, mr * wi + mi * wr
            y_ref[0:32, lanes] = (hwr * mr - hwi * mi).astype(BF16)
            y_ref[32:64, lanes] = (gr * hwr + gi * hwi).astype(BF16)
            y_ref[64:96, lanes] = (gr * mwr + gi * mwi).astype(BF16)
            imag = jnp.concatenate(
                [hwr * mi + hwi * mr, gi * hwr - gr * hwi, gi * mwr - gr * mwi], axis=0
            ).astype(BF16)
            for b in range(chunk // 256):
                at = SEQ - (n * chunk + (b + 1) * 256)
                y_ref[96:192, pl.ds(at, 256)] = dot(imag[:, b * 256 : (b + 1) * 256], rev).astype(BF16)
        scale = 1.0 / SEQ
        for n in range(n_chunks):
            lanes = pl.ds(n * chunk, chunk)
            back = dot(y_ref[...], m_ref[:, lanes])
            back = (back[0:96] - back[96:192] * w_ref[2:3, lanes]) * scale
            for b in range(chunk // 128):
                at = n * (chunk // 128) + b
                part = r_ref[at]
                cut = slice(b * 128, (b + 1) * 128)
                conv, mixed, raw = back[0:32, cut], back[32:64, cut], back[64:96, cut]
                query, key, value, gate = (part[32 * i : 32 * i + 32].astype(F32) for i in range(4))
                gq = (gate * conv).astype(BF16)
                gk = (mixed * value).astype(BF16)
                gv = (mixed * key).astype(BF16)
                pos = pl.ds((at % 2 * 8 + at // 2) * 128, 128)
                b_ref[0:32, pos] = gq
                b_ref[32:64, pos] = gk
                b_ref[64:96, pos] = gv
                b_ref[96:128, pos] = (query * conv).astype(BF16)
                o_ref[at, 0:32, :] = gq
                o_ref[at, 32:64, :] = gk
                o_ref[at, 64:96, :] = gv
                raw = raw * (1.0 / math.sqrt(SEQ))
                high = raw.astype(BF16)
                o_ref[at, 96:128, :] = high
                o_ref[at, 128:160, :] = (raw - high.astype(F32)).astype(BF16)

    vm = pl.BlockSpec(memory_space=pltpu.VMEM)
    return call(
        kernel,
        in_specs=[vm, pl.BlockSpec(memory_space=pl.ANY), vm, vm],
        out_specs=[vm, vm, vm],
        out_shape=[
            jax.ShapeDtypeStruct((128, SEQ), BF16),
            jax.ShapeDtypeStruct((16, 160, 128), BF16),
            jax.ShapeDtypeStruct((16, SEQ_DEV, 128), BF16),
        ],
        scratch_shapes=[
            pltpu.VMEM((SEQ, SEQ), BF16),
            pltpu.VMEM((192, SEQ), BF16),
            pltpu.VMEM((192, SEQ), BF16),
            pltpu.SemaphoreType.DMA((n_chunks,)),
        ],
        flops=4 * 192 * SEQ * SEQ,
        bytes_accessed=12 * MIB,
        vmem=20,
        name="convolve",
    )(received, in_hbm(matrix), rows, flip)


def input_partial(received, weight):
    steps = 8
    depth = 4096 // steps

    def kernel(r_ref, w_hbm, o_ref, f_ref, w_ref, g_ref, sem):
        groups = []
        for s in range(steps):
            rows = pl.ds(s * depth, depth)
            groups.append(
                [
                    pltpu.make_async_copy(w_hbm.at[j, rows], w_ref.at[rows, pl.ds(j * 512, 512)], sem.at[s, j])
                    for j in range(3)
                ]
            )
        stream = Stream(groups, steps)
        for chip in range(8):
            for core in range(2):
                at = core * 256 + chip * BLOCK
                for j in range(5):
                    g_ref[j * 512 + at : j * 512 + at + BLOCK, :] = r_ref[
                        2 * chip + core, j * BLOCK : (j + 1) * BLOCK, :
                    ]
        grads = g_ref[0:1536].astype(F32).T.astype(BF16)
        f_ref[...] = (g_ref[1536:2048].astype(F32) + g_ref[2048:2560].astype(F32)).T
        for s in range(steps):
            stream.wait(s)
            o_ref[s] = dot(grads, w_ref[s * depth : (s + 1) * depth], NT).astype(BF16)

    vm = pl.BlockSpec(memory_space=pltpu.VMEM)
    return call(
        kernel,
        in_specs=[vm, pl.BlockSpec(memory_space=pl.ANY)],
        out_specs=[vm, vm],
        out_shape=[
            jax.ShapeDtypeStruct((8, SEQ_DEV, 512), BF16),
            jax.ShapeDtypeStruct((SEQ_DEV, 512), F32),
        ],
        scratch_shapes=[
            pltpu.VMEM((4096, 1536), BF16),
            pltpu.VMEM((2560, SEQ_DEV), BF16),
            pltpu.SemaphoreType.DMA((steps, 3)),
        ],
        flops=2 * 128 * 4096 * 1536,
        bytes_accessed=14 * MIB,
        vmem=24,
        name="input_partial",
    )(received, in_hbm(weight))


def sum_partials(parts):
    def kernel(p_ref, o_ref):
        total = p_ref[0].astype(F32)
        for i in range(1, 8):
            total = total + p_ref[i].astype(F32)
        o_ref[...] = total.astype(BF16)

    vm = pl.BlockSpec(memory_space=pltpu.VMEM)
    return call(
        kernel,
        in_specs=[vm],
        out_specs=vm,
        out_shape=jax.ShapeDtypeStruct((SEQ_DEV, 512), BF16),
        bytes_accessed=MIB,
        name="sum_partials",
    )(parts)


def pair(first, second, third, fourth):
    def kernel(a, b, c, d, o_ref, p_ref, sem):
        copies = []
        for i, (src, out) in enumerate(((a, o_ref), (b, o_ref), (c, p_ref), (d, p_ref))):
            copies.append(pltpu.make_async_copy(src, out.at[pl.ds(i % 2 * 128, 128)], sem.at[i]))
        for copy in copies:
            copy.start()
        for copy in copies:
            copy.wait()

    hbm = pl.BlockSpec(memory_space=pl.ANY)
    return call(
        kernel,
        in_specs=[hbm] * 4,
        out_specs=[pl.BlockSpec(memory_space=pltpu.VMEM)] * 2,
        out_shape=[jax.ShapeDtypeStruct((256, SEQ), BF16)] * 2,
        scratch_shapes=[pltpu.SemaphoreType.DMA((4,))],
        vmem=4,
        name="pair",
    )(first, second, third, fourth)


def weight_gradients(place, columns, blocks):
    factor = 1.0 / math.sqrt(SEQ)
    first_rows = [first for _, first in blocks]

    def kernel(place_ref, *refs):
        column_refs, block_refs = refs[:8], refs[8:16]
        in_hbm, out_hbm, send_ref, t_ref, g_ref, res_ref, t_sem, sem, out_sem = refs[16:]
        core = place_ref[8]
        t_copies = []
        for i in range(8):
            lanes = pl.ds(pl.multiple_of(place_ref[9 + i % 4] * 128, 128), 128)
            kind = core if i < 4 else 1 - core
            for c in range(2):
                src = column_refs[i].at[:, c]
                t_copies.append(pltpu.make_async_copy(src, t_ref.at[kind, c, :, :, lanes], t_sem.at[c, i]))
        copies = [[], [], [], []]
        for j in range(4):
            for k in range(8):
                at = pl.multiple_of(place_ref[k] * BLOCK, BLOCK)
                copies[j].append(
                    pltpu.make_async_copy(
                        block_refs[k].at[pl.ds(first_rows[k] + j * BLOCK, BLOCK)], g_ref.at[j, pl.ds(at, BLOCK)], sem.at[j, k]
                    )
                )
        for copy in t_copies + copies[0] + copies[1] + copies[2] + copies[3]:
            copy.start()
        half = pl.multiple_of(core * 256, 256)
        rest = pl.multiple_of((1 - core) * 256, 256)
        outs = []
        for j in range(4):
            for copy in copies[j] + (t_copies if j == 0 else []):
                copy.wait()
            total = dot(g_ref[j], t_ref[j // 3].reshape(SEQ, 512))
            total = total * factor
            if j < 3:
                res_ref[j] = total.T
                send_ref[j * 256 : (j + 1) * 256, :] = res_ref[j, pl.ds(rest, 256), :].astype(BF16)
                src, dst = res_ref.at[j, pl.ds(half, 256)], in_hbm.at[j, :, pl.ds(half, 256)]
            else:
                res_ref[3, 0:256] = total[:, 0:256]
                res_ref[3, 256:512] = total[:, 256:512]
                send_ref[768:1024, :] = res_ref[3, pl.ds(rest, 256), :].astype(BF16)
                src, dst = res_ref.at[3, pl.ds(half, 256)], out_hbm.at[pl.ds(half, 256)]
            outs.append(pltpu.make_async_copy(src, dst, out_sem.at[j]))
            outs[-1].start()
        for copy in outs:
            copy.wait()

    vm = pl.BlockSpec(memory_space=pltpu.VMEM)
    hbm = pl.BlockSpec(memory_space=pl.ANY)
    return call(
        kernel,
        in_specs=[pl.BlockSpec(memory_space=pltpu.SMEM)] + [hbm] * 16,
        out_specs=[hbm, hbm, vm],
        out_shape=[
            jax.ShapeDtypeStruct((3, 256, 512), F32),
            jax.ShapeDtypeStruct((512, 256), F32),
            jax.ShapeDtypeStruct((1024, 256), BF16),
        ],
        scratch_shapes=[
            pltpu.VMEM((2, 2, 8, SEQ_DEV, 512), BF16),
            pltpu.VMEM((4, 256, SEQ), BF16),
            pltpu.VMEM((4, 512, 256), F32),
            pltpu.SemaphoreType.DMA((2, 8)),
            pltpu.SemaphoreType.DMA((4, 8)),
            pltpu.SemaphoreType.DMA((4,)),
        ],
        vmem=24,
        name="weight_gradients",
    )(place, *[in_hbm(value.reshape(8, 2, SEQ_DEV, 128)) for value in columns], *[in_hbm(block) for block, _ in blocks])


def fill_halves(place, sent, in_grad, out_grad):
    def kernel(place_ref, s_ref, in_old, out_old, in_hbm, out_hbm, res_ref, sem):
        half = pl.multiple_of((1 - place_ref[8]) * 256, 256)
        outs = []
        for j in range(4):
            res_ref[j] = s_ref[j * 256 : (j + 1) * 256, :].astype(F32)
            dst = in_hbm.at[j, :, pl.ds(half, 256)] if j < 3 else out_hbm.at[pl.ds(half, 256)]
            outs.append(pltpu.make_async_copy(res_ref.at[j], dst, sem.at[j]))
            outs[-1].start()
        for copy in outs:
            copy.wait()

    vm = pl.BlockSpec(memory_space=pltpu.VMEM)
    hbm = pl.BlockSpec(memory_space=pl.ANY)
    return call(
        kernel,
        in_specs=[pl.BlockSpec(memory_space=pltpu.SMEM), vm, hbm, hbm],
        out_specs=[hbm, hbm],
        out_shape=[jax.ShapeDtypeStruct((3, 256, 512), F32), jax.ShapeDtypeStruct((512, 256), F32)],
        scratch_shapes=[pltpu.VMEM((4, 256, 256), F32), pltpu.SemaphoreType.DMA((4,))],
        input_output_aliases={2: 0, 3: 1},
        vmem=8,
        name="fill_halves",
    )(place, sent, in_hbm(in_grad), in_hbm(out_grad))


def chip_hop(x_flip, z_step):
    pairs = []
    for i in range(16):
        x, z, core = i // 8, i // 2 % 4, i % 2
        pairs.append((i, ((x ^ x_flip) * 4 + (z + z_step) % 4) * 2 + core))
    return pairs


def swap_cores(value):
    return lax.ppermute(value, "ctx", [(i, i ^ 1) for i in range(16)])


def swap(pieces, axis, groups=None):
    return lax.all_to_all(pieces, axis, 0, 0, axis_index_groups=groups, tiled=True)


HOPS = ((0, 0), (0, 1), (0, 3), (1, 0), (0, 2), (1, 1), (1, 3), (1, 2))


def hop(value, x_flip, z_step):
    return lax.ppermute(value, "ctx", chip_hop(x_flip, z_step))


def after(value, *others):
    return lax.optimization_barrier((value,) + others)[0]


def hop_y(value, step):
    return lax.ppermute(value, "mp", [(i, i // 4 * 4 + (i % 4 + step) % 4) for i in range(8)])


def on_device(tokens, out_grad, in_weight, out_weight, filters):
    position = lax.axis_index("ctx")
    core, x, z = position & 1, position >> 3, (position >> 1) & 3
    y = lax.axis_index("mp") & 3
    place = [((x ^ f) << 2) + ((z - s) & 3) for f, s in HOPS] + [core] + [(y - s) & 3 for s in range(4)]
    place = jnp.stack(place).astype(jnp.int32)
    weight = jnp.transpose(in_weight, (1, 0, 2))
    signals = project(y.astype(jnp.int32)[None], tokens, out_grad, weight, out_weight, filters)
    signals = swap(signals.reshape(16, 5 * BLOCK + 128, SEQ_DEV), "ctx")
    flip = jnp.asarray(np.eye(256)[::-1].astype(ml_dtypes.bfloat16))
    block, pieces, columns = convolve(
        signals, jnp.asarray(cosine_matrix()), jnp.asarray(frequency_rows()), flip
    )
    columns = [columns] + [hop_y(columns, s) for s in (1, 2, 3)]
    up, down, flipped = hop(block, 0, 1), hop(block, 0, 3), hop(block, 1, 0)
    pieces = swap(pieces, "ctx")
    up, down, flipped, pieces = lax.optimization_barrier((up, down, flipped, pieces))
    near, here = pair(up, down, block, flipped)
    across, two = hop(near, 1, 0), hop(here, 0, 2)
    pieces = after(pieces, near)
    partial, filter_grad = input_partial(pieces, weight)
    parts = swap(partial, "mp")
    columns = columns[:2] + [after(value, partial) for value in columns[2:]]
    columns += [swap_cores(value) for value in columns]
    input_grad = sum_partials(parts)
    blocks = [(block, 0), (up, 0), (down, 0), (flipped, 0), (two, 0), (across, 0), (across, 128), (two, 128)]
    in_grad, out_weight_grad, send = weight_gradients(place, columns, blocks)
    in_grad, out_weight_grad = fill_halves(place, swap_cores(send), in_grad, out_weight_grad)
    return (input_grad, jnp.transpose(in_grad, (1, 0, 2)), out_weight_grad, filter_grad)


def solution(mesh):
    in_specs = (P("ctx", None), P("ctx", None), P(None, None, "mp"), P("mp", None), P("ctx", "mp"))
    out_specs = (P("ctx", "mp"), P("ctx", None, "mp"), P("mp", "ctx"), P("ctx", "mp"))
    return jax.shard_map(
        on_device, mesh=mesh, in_specs=in_specs, out_specs=out_specs, check_vma=False
    )
```

```python
import math

import jax
import jax.numpy as jnp
import ml_dtypes
import numpy as np
from jax import lax
from jax.experimental import pallas as pl
from jax.experimental.pallas import tpu as pltpu
from jax.sharding import PartitionSpec as P

F32 = jnp.float32
BF16 = jnp.bfloat16
NT = (((1,), (1,)), ((), ()))
NN = (((1,), (0,)), ((), ()))
MIB = 1 << 20
BLOCK = 32
SEQ_DEV = 128
SEQ = 2048


def dot(a, b, dims=NN):
    return lax.dot_general(a, b, dims, preferred_element_type=F32)


def in_hbm(value):
    return pltpu.with_memory_space_constraint(value, pltpu.HBM)


def in_vmem(value):
    return pltpu.with_memory_space_constraint(value, pltpu.VMEM)


class Stream:
    def __init__(self, groups, ahead):
        self.groups, self.started, self.ahead = groups, 0, ahead
        self.start(ahead)

    def start(self, upto):
        while self.started < min(upto, len(self.groups)):
            for copy in self.groups[self.started]:
                copy.start()
            self.started += 1

    def wait(self, index):
        for copy in self.groups[index]:
            copy.wait()
        self.start(index + 1 + self.ahead)


def call(kernel, *, flops=0, bytes_accessed=0, vmem=32, **kw):
    return pl.pallas_call(
        kernel,
        compiler_params=pltpu.CompilerParams(vmem_limit_bytes=vmem * MIB),
        cost_estimate=pl.CostEstimate(flops=flops, bytes_accessed=bytes_accessed, transcendentals=0),
        **kw,
    )


def project(quarter, tokens, out_grad, weight, out_weight, filters):
    depth = 2048
    steps = 4096 // depth
    gate = 256

    def kernel(y_ref, t_hbm, g_hbm, f_hbm, w_hbm, ow_hbm, o_ref, f_ref, t_ref, g_ref, w_ref, ow_ref, sem):
        def fetch(src, dst, at):
            return pltpu.make_async_copy(src, dst, sem.at[at])

        gates = [pl.ds(gate * i, gate) for i in range(512 // gate)]
        groups = [[fetch(ow_hbm.at[rows], ow_ref.at[rows], i)] for i, rows in enumerate(gates)]
        first = len(groups)
        groups[0] = [fetch(f_hbm, f_ref, first), fetch(g_hbm, g_ref, first + 1)] + groups[0]
        for j in range(3):
            for k in range(steps):
                rows = pl.ds(k * depth, depth)
                at = first + 3 + j * steps + k
                groups.append([fetch(w_hbm.at[j, rows], w_ref.at[j, rows], at)])
        groups[first].append(fetch(t_hbm, t_ref, first + 2))
        stream = Stream(groups, 8)

        def put(first, sig, rows):
            n = rows.shape[0] // BLOCK
            core, chip = first // 256, first % 256 // BLOCK
            o_ref[chip : chip + n, core, sig * BLOCK : (sig + 1) * BLOCK, :] = rows.astype(BF16).reshape(
                n, BLOCK, SEQ_DEV
            )

        for i in range(512 // gate):
            stream.wait(i)
            put(i * gate, 3, dot(ow_ref[i * gate : (i + 1) * gate], g_ref[...], NT))
        for c in range(2):
            put(c * 256, 4, f_ref[:, c * 256 : (c + 1) * 256].T)
        for chip in range(8):
            lanes = pl.ds(pl.multiple_of(chip * 512 + y_ref[0] * 128, 128), 128)
            o_ref[chip, 1, 5 * BLOCK :, :] = g_ref[:, lanes]
        for j in range(3):
            total = None
            for k in range(steps):
                stream.wait(first + j * steps + k)
                part = dot(t_ref[:, k * depth : (k + 1) * depth], w_ref[j, k * depth : (k + 1) * depth])
                total = part if total is None else total + part
            if j == 0:
                for chip in range(8):
                    lanes = pl.ds(pl.multiple_of(chip * 512 + y_ref[0] * 128, 128), 128)
                    o_ref[chip, 0, 5 * BLOCK :, :] = t_ref[:, lanes]
            for c in range(2):
                put(c * 256, j, total[:, c * 256 : (c + 1) * 256].T)

    vm = pl.BlockSpec(memory_space=pltpu.VMEM)
    hbm = pl.BlockSpec(memory_space=pl.ANY)
    return call(
        kernel,
        in_specs=[pl.BlockSpec(memory_space=pltpu.SMEM)] + [hbm] * 5,
        out_specs=vm,
        out_shape=jax.ShapeDtypeStruct((8, 2, 5 * BLOCK + 128, SEQ_DEV), BF16),
        scratch_shapes=[
            pltpu.VMEM((SEQ_DEV, 512), F32),
            pltpu.VMEM((SEQ_DEV, 4096), BF16),
            pltpu.VMEM((SEQ_DEV, 4096), BF16),
            pltpu.VMEM((3, 4096, 512), BF16),
            pltpu.VMEM((512, 4096), BF16),
            pltpu.SemaphoreType.DMA((3 + 512 // gate + 3 * steps,)),
        ],
        flops=2 * 128 * 4096 * 2048,
        bytes_accessed=19 * MIB,
        vmem=28,
        name="project",
    )(quarter, in_hbm(tokens), in_hbm(out_grad), in_hbm(filters), in_hbm(weight), in_hbm(out_weight))


def cosine_matrix():
    odd = 2 * np.arange(SEQ, dtype=np.int64) + 1
    turns = np.outer(odd, odd) % (8 * SEQ)
    return np.cos(turns * (2.0 * np.pi / (8 * SEQ))).astype(ml_dtypes.bfloat16)


def frequency_rows():
    half = (2 * np.arange(SEQ) + 1) * (np.pi / (4 * SEQ))
    sign = 1.0 - 2.0 * (np.arange(SEQ) % 2)
    rows = np.zeros((8, SEQ), np.float32)
    rows[0], rows[1], rows[2] = np.cos(half), np.sin(half), sign
    return rows


def convolve(received, matrix, rows, flip):
    chunk = 512
    n_chunks = SEQ // chunk

    def kernel(r_ref, m_ref, w_ref, j_ref, b_ref, o_ref, c_ref, x_ref, y_ref):
        rev = j_ref[...]
        c_ref[...] = r_ref[:, 5 * BLOCK :, :].reshape(8, 2, SEQ_DEV, 128)
        for b in range(16):
            part = r_ref[b]
            key, value = part[32:64].astype(F32), part[64:96].astype(F32)
            query, gate = part[0:32].astype(F32), part[96:128].astype(F32)
            lanes = pl.ds(b * 128, 128)
            x_ref[0:32, lanes] = part[128:160]
            x_ref[32:64, lanes] = (key * value).astype(BF16)
            x_ref[64:96, lanes] = (gate * query).astype(BF16)
        for b in range(8):
            x_ref[96:192, pl.ds((7 - b) * 256, 256)] = dot(x_ref[0:96, pl.ds(b * 256, 256)], rev).astype(BF16)
        for n in range(n_chunks):
            lanes = pl.ds(n * chunk, chunk)
            spec = dot(x_ref[...], m_ref[:, lanes])
            wr, wi, sign = w_ref[0:1, lanes], w_ref[1:2, lanes], w_ref[2:3, lanes]
            hr, mr, gr = spec[0:32], spec[32:64], spec[64:96]
            neg = -sign
            hi, mi, gi = spec[96:128] * neg, spec[128:160] * neg, spec[160:192] * neg
            hwr, hwi = hr * wr - hi * wi, hr * wi + hi * wr
            mwr, mwi = mr * wr - mi * wi, mr * wi + mi * wr
            y_ref[0:32, lanes] = (hwr * mr - hwi * mi).astype(BF16)
            y_ref[32:64, lanes] = (gr * hwr + gi * hwi).astype(BF16)
            y_ref[64:96, lanes] = (gr * mwr + gi * mwi).astype(BF16)
            imag = jnp.concatenate(
                [hwr * mi + hwi * mr, gi * hwr - gr * hwi, gi * mwr - gr * mwi], axis=0
            ).astype(BF16)
            for b in range(chunk // 256):
                at = SEQ - (n * chunk + (b + 1) * 256)
                y_ref[96:192, pl.ds(at, 256)] = dot(imag[:, b * 256 : (b + 1) * 256], rev).astype(BF16)
        scale = 1.0 / SEQ
        for n in range(n_chunks):
            lanes = pl.ds(n * chunk, chunk)
            back = dot(y_ref[...], m_ref[:, lanes])
            back = (back[0:96] - back[96:192] * w_ref[2:3, lanes]) * scale
            for b in range(chunk // 128):
                at = n * (chunk // 128) + b
                part = r_ref[at]
                cut = slice(b * 128, (b + 1) * 128)
                conv, mixed, raw = back[0:32, cut], back[32:64, cut], back[64:96, cut]
                query, key, value, gate = (part[32 * i : 32 * i + 32].astype(F32) for i in range(4))
                gq = (gate * conv).astype(BF16)
                gk = (mixed * value).astype(BF16)
                gv = (mixed * key).astype(BF16)
                pos = pl.ds((at % 2 * 8 + at // 2) * 128, 128)
                b_ref[0:32, pos] = gq
                b_ref[32:64, pos] = gk
                b_ref[64:96, pos] = gv
                b_ref[96:128, pos] = (query * conv).astype(BF16)
                o_ref[at, 0:32, :] = gq
                o_ref[at, 32:64, :] = gk
                o_ref[at, 64:96, :] = gv
                raw = raw * (1.0 / math.sqrt(SEQ))
                high = raw.astype(BF16)
                o_ref[at, 96:128, :] = high
                o_ref[at, 128:160, :] = (raw - high.astype(F32)).astype(BF16)

    vm = pl.BlockSpec(memory_space=pltpu.VMEM)
    return call(
        kernel,
        in_specs=[vm, vm, vm, vm],
        out_specs=[vm, vm, vm],
        out_shape=[
            jax.ShapeDtypeStruct((128, SEQ), BF16),
            jax.ShapeDtypeStruct((16, 160, 128), BF16),
            jax.ShapeDtypeStruct((8, 2, SEQ_DEV, 128), BF16),
        ],
        scratch_shapes=[
            pltpu.VMEM((192, SEQ), BF16),
            pltpu.VMEM((192, SEQ), BF16),
        ],
        flops=4 * 192 * SEQ * SEQ,
        bytes_accessed=12 * MIB,
        vmem=20,
        name="convolve",
    )(received, in_vmem(matrix), rows, flip)


def input_partial(received, weight):
    steps = 8
    depth = 4096 // steps

    def kernel(r_ref, w_hbm, o_ref, f_ref, w_ref, g_ref, sem):
        groups = []
        for s in range(steps):
            rows = pl.ds(s * depth, depth)
            groups.append(
                [
                    pltpu.make_async_copy(w_hbm.at[j, rows], w_ref.at[rows, pl.ds(j * 512, 512)], sem.at[s, j])
                    for j in range(3)
                ]
            )
        stream = Stream(groups, steps)
        for chip in range(8):
            for core in range(2):
                at = core * 256 + chip * BLOCK
                for j in range(5):
                    g_ref[j * 512 + at : j * 512 + at + BLOCK, :] = r_ref[
                        2 * chip + core, j * BLOCK : (j + 1) * BLOCK, :
                    ]
        grads = g_ref[0:1536].astype(F32).T.astype(BF16)
        f_ref[...] = (g_ref[1536:2048].astype(F32) + g_ref[2048:2560].astype(F32)).T
        for s in range(steps):
            stream.wait(s)
            o_ref[s] = dot(grads, w_ref[s * depth : (s + 1) * depth], NT).astype(BF16)

    vm = pl.BlockSpec(memory_space=pltpu.VMEM)
    return call(
        kernel,
        in_specs=[vm, pl.BlockSpec(memory_space=pl.ANY)],
        out_specs=[vm, vm],
        out_shape=[
            jax.ShapeDtypeStruct((8, SEQ_DEV, 512), BF16),
            jax.ShapeDtypeStruct((SEQ_DEV, 512), F32),
        ],
        scratch_shapes=[
            pltpu.VMEM((4096, 1536), BF16),
            pltpu.VMEM((2560, SEQ_DEV), BF16),
            pltpu.SemaphoreType.DMA((steps, 3)),
        ],
        flops=2 * 128 * 4096 * 1536,
        bytes_accessed=14 * MIB,
        vmem=24,
        name="input_partial",
    )(received, in_hbm(weight))


def sum_partials(parts):
    def kernel(p_ref, o_ref):
        total = p_ref[0].astype(F32)
        for i in range(1, 8):
            total = total + p_ref[i].astype(F32)
        o_ref[...] = total.astype(BF16)

    vm = pl.BlockSpec(memory_space=pltpu.VMEM)
    return call(
        kernel,
        in_specs=[vm],
        out_specs=vm,
        out_shape=jax.ShapeDtypeStruct((SEQ_DEV, 512), BF16),
        bytes_accessed=MIB,
        name="sum_partials",
    )(parts)


def pair(first, second, third, fourth):
    def kernel(a, b, c, d, o_ref, p_ref, sem):
        copies = []
        for i, (src, out) in enumerate(((a, o_ref), (b, o_ref), (c, p_ref), (d, p_ref))):
            copies.append(pltpu.make_async_copy(src, out.at[pl.ds(i % 2 * 128, 128)], sem.at[i]))
        for copy in copies:
            copy.start()
        for copy in copies:
            copy.wait()

    hbm = pl.BlockSpec(memory_space=pl.ANY)
    return call(
        kernel,
        in_specs=[hbm] * 4,
        out_specs=[pl.BlockSpec(memory_space=pltpu.VMEM)] * 2,
        out_shape=[jax.ShapeDtypeStruct((256, SEQ), BF16)] * 2,
        scratch_shapes=[pltpu.SemaphoreType.DMA((4,))],
        vmem=4,
        name="pair",
    )(first, second, third, fourth)


def weight_gradients(place, columns, blocks):
    factor = 1.0 / math.sqrt(SEQ)
    first_rows = [first for _, first in blocks]

    def kernel(place_ref, *refs):
        column_refs, block_refs = refs[:8], refs[8:16]
        in_hbm, out_hbm, send_ref, t_ref, g_ref, res_ref, t_sem, sem, out_sem = refs[16:]
        core = place_ref[8]
        t_copies = []
        for i in range(8):
            lanes = pl.ds(pl.multiple_of(place_ref[9 + i % 4] * 128, 128), 128)
            kind = core if i < 4 else 1 - core
            for c in range(2):
                src = column_refs[i].at[:, c]
                t_copies.append(pltpu.make_async_copy(src, t_ref.at[kind, c, :, :, lanes], t_sem.at[c, i]))
        copies = [[], [], [], []]
        for j in range(4):
            for k in range(8):
                at = pl.multiple_of(place_ref[k] * BLOCK, BLOCK)
                copies[j].append(
                    pltpu.make_async_copy(
                        block_refs[k].at[pl.ds(first_rows[k] + j * BLOCK, BLOCK)], g_ref.at[j, pl.ds(at, BLOCK)], sem.at[j, k]
                    )
                )
        for copy in t_copies + copies[0] + copies[1] + copies[2] + copies[3]:
            copy.start()
        half = pl.multiple_of(core * 256, 256)
        rest = pl.multiple_of((1 - core) * 256, 256)
        outs = []
        for j in range(4):
            for copy in copies[j] + (t_copies if j == 0 else []):
                copy.wait()
            total = dot(g_ref[j], t_ref[j // 3].reshape(SEQ, 512))
            total = total * factor
            if j < 3:
                res_ref[j] = total.T
                send_ref[j * 256 : (j + 1) * 256, :] = res_ref[j, pl.ds(rest, 256), :].astype(BF16)
                src, dst = res_ref.at[j, pl.ds(half, 256)], in_hbm.at[j, :, pl.ds(half, 256)]
            else:
                res_ref[3, 0:256] = total[:, 0:256]
                res_ref[3, 256:512] = total[:, 256:512]
                send_ref[768:1024, :] = res_ref[3, pl.ds(rest, 256), :].astype(BF16)
                src, dst = res_ref.at[3, pl.ds(half, 256)], out_hbm.at[pl.ds(half, 256)]
            outs.append(pltpu.make_async_copy(src, dst, out_sem.at[j]))
            outs[-1].start()
        for copy in outs:
            copy.wait()

    vm = pl.BlockSpec(memory_space=pltpu.VMEM)
    hbm = pl.BlockSpec(memory_space=pl.ANY)
    return call(
        kernel,
        in_specs=[pl.BlockSpec(memory_space=pltpu.SMEM)] + [hbm] * 16,
        out_specs=[hbm, hbm, vm],
        out_shape=[
            jax.ShapeDtypeStruct((3, 256, 512), F32),
            jax.ShapeDtypeStruct((512, 256), F32),
            jax.ShapeDtypeStruct((1024, 256), BF16),
        ],
        scratch_shapes=[
            pltpu.VMEM((2, 2, 8, SEQ_DEV, 512), BF16),
            pltpu.VMEM((4, 256, SEQ), BF16),
            pltpu.VMEM((4, 512, 256), F32),
            pltpu.SemaphoreType.DMA((2, 8)),
            pltpu.SemaphoreType.DMA((4, 8)),
            pltpu.SemaphoreType.DMA((4,)),
        ],
        vmem=24,
        name="weight_gradients",
    )(place, columns[0], *map(in_hbm, columns[1:]), blocks[0][0], *[in_hbm(block) for block, _ in blocks[1:]])


def fill_halves(place, sent, in_grad, out_grad):
    def kernel(place_ref, s_ref, in_old, out_old, in_hbm, out_hbm, res_ref, sem):
        half = pl.multiple_of((1 - place_ref[8]) * 256, 256)
        outs = []
        for j in range(4):
            res_ref[j] = s_ref[j * 256 : (j + 1) * 256, :].astype(F32)
            dst = in_hbm.at[j, :, pl.ds(half, 256)] if j < 3 else out_hbm.at[pl.ds(half, 256)]
            outs.append(pltpu.make_async_copy(res_ref.at[j], dst, sem.at[j]))
            outs[-1].start()
        for copy in outs:
            copy.wait()

    vm = pl.BlockSpec(memory_space=pltpu.VMEM)
    hbm = pl.BlockSpec(memory_space=pl.ANY)
    return call(
        kernel,
        in_specs=[pl.BlockSpec(memory_space=pltpu.SMEM), vm, hbm, hbm],
        out_specs=[hbm, hbm],
        out_shape=[jax.ShapeDtypeStruct((3, 256, 512), F32), jax.ShapeDtypeStruct((512, 256), F32)],
        scratch_shapes=[pltpu.VMEM((4, 256, 256), F32), pltpu.SemaphoreType.DMA((4,))],
        input_output_aliases={2: 0, 3: 1},
        vmem=8,
        name="fill_halves",
    )(place, sent, in_hbm(in_grad), in_hbm(out_grad))


def chip_hop(x_flip, z_step):
    pairs = []
    for i in range(16):
        x, z, core = i // 8, i // 2 % 4, i % 2
        pairs.append((i, ((x ^ x_flip) * 4 + (z + z_step) % 4) * 2 + core))
    return pairs


def swap_cores(value):
    return lax.ppermute(value, "ctx", [(i, i ^ 1) for i in range(16)])


def swap(pieces, axis, groups=None):
    return lax.all_to_all(pieces, axis, 0, 0, axis_index_groups=groups, tiled=True)


HOPS = ((0, 0), (0, 1), (0, 3), (1, 0), (0, 2), (1, 1), (1, 3), (1, 2))


def hop(value, x_flip, z_step):
    return lax.ppermute(value, "ctx", chip_hop(x_flip, z_step))


def after(value, *others):
    return lax.optimization_barrier((value,) + others)[0]


def hop_y(value, step):
    return lax.ppermute(value, "mp", [(i, i // 4 * 4 + (i % 4 + step) % 4) for i in range(8)])


def on_device(tokens, out_grad, in_weight, out_weight, filters):
    position = lax.axis_index("ctx")
    core, x, z = position & 1, position >> 3, (position >> 1) & 3
    y = lax.axis_index("mp") & 3
    place = [((x ^ f) << 2) + ((z - s) & 3) for f, s in HOPS] + [core] + [(y - s) & 3 for s in (0, 1, 3, 2)]
    place = jnp.stack(place).astype(jnp.int32)
    weight = jnp.transpose(in_weight, (1, 0, 2))
    signals = project(y.astype(jnp.int32)[None], tokens, out_grad, weight, out_weight, filters)
    signals = swap(signals.reshape(16, 5 * BLOCK + 128, SEQ_DEV), "ctx")
    flip = jnp.asarray(np.eye(256)[::-1].astype(ml_dtypes.bfloat16))
    block, pieces, columns = convolve(
        signals, jnp.asarray(cosine_matrix()), jnp.asarray(frequency_rows()), flip
    )
    columns = [columns] + [hop_y(columns, s) for s in (1, 3, 2)]
    up, down, flipped = hop(block, 0, 1), hop(block, 0, 3), hop(block, 1, 0)
    pieces = swap(pieces, "ctx")
    up, down, flipped, pieces = lax.optimization_barrier((up, down, flipped, pieces))
    near, here = pair(up, down, block, flipped)
    across, two = hop(near, 1, 0), hop(here, 0, 2)
    pieces = after(pieces, near)
    partial, filter_grad = input_partial(pieces, weight)
    parts = swap(partial, "mp")
    columns = columns[:2] + [after(value, partial) for value in columns[2:]]
    columns += [swap_cores(value) for value in columns]
    input_grad = sum_partials(parts)
    blocks = [(block, 0), (up, 0), (down, 0), (flipped, 0), (two, 0), (across, 0), (across, 128), (two, 128)]
    in_grad, out_weight_grad, send = weight_gradients(place, columns, blocks)
    in_grad, out_weight_grad = fill_halves(place, swap_cores(send), in_grad, out_weight_grad)
    return (input_grad, jnp.transpose(in_grad, (1, 0, 2)), out_weight_grad, filter_grad)


def solution(mesh):
    in_specs = (P("ctx", None), P("ctx", None), P(None, None, "mp"), P("mp", None), P("ctx", "mp"))
    out_specs = (P("ctx", "mp"), P("ctx", None, "mp"), P("mp", "ctx"), P("ctx", "mp"))
    return jax.shard_map(
        on_device, mesh=mesh, in_specs=in_specs, out_specs=out_specs, check_vma=False
    )
```

```python
import math

import jax
import jax.numpy as jnp
import ml_dtypes
import numpy as np
from jax import lax
from jax.experimental import pallas as pl
from jax.experimental.pallas import tpu as pltpu
from jax.sharding import PartitionSpec as P

F32 = jnp.float32
BF16 = jnp.bfloat16
NT = (((1,), (1,)), ((), ()))
NN = (((1,), (0,)), ((), ()))
MIB = 1 << 20
BLOCK = 32
SEQ_DEV = 128
SEQ = 2048


def dot(a, b, dims=NN):
    return lax.dot_general(a, b, dims, preferred_element_type=F32)


def in_hbm(value):
    return pltpu.with_memory_space_constraint(value, pltpu.HBM)


def in_vmem(value):
    return pltpu.with_memory_space_constraint(value, pltpu.VMEM)


class Stream:
    def __init__(self, groups, ahead):
        self.groups, self.started, self.ahead = groups, 0, ahead
        self.start(ahead)

    def start(self, upto):
        while self.started < min(upto, len(self.groups)):
            for copy in self.groups[self.started]:
                copy.start()
            self.started += 1

    def wait(self, index):
        for copy in self.groups[index]:
            copy.wait()
        self.start(index + 1 + self.ahead)


def call(kernel, *, flops=0, bytes_accessed=0, vmem=32, **kw):
    return pl.pallas_call(
        kernel,
        compiler_params=pltpu.CompilerParams(vmem_limit_bytes=vmem * MIB),
        cost_estimate=pl.CostEstimate(flops=flops, bytes_accessed=bytes_accessed, transcendentals=0),
        **kw,
    )


def project(quarter, tokens, out_grad, weight, out_weight, filters):
    depth = 2048
    steps = 4096 // depth
    gate = 256

    def kernel(y_ref, t_hbm, g_hbm, f_hbm, w_hbm, ow_hbm, o_ref, f_ref, t_ref, g_ref, w_ref, ow_ref, sem):
        def fetch(src, dst, at):
            return pltpu.make_async_copy(src, dst, sem.at[at])

        gates = [pl.ds(gate * i, gate) for i in range(512 // gate)]
        groups = [[fetch(ow_hbm.at[rows], ow_ref.at[rows], i)] for i, rows in enumerate(gates)]
        first = len(groups)
        groups[0] = [fetch(f_hbm, f_ref, first), fetch(g_hbm, g_ref, first + 1)] + groups[0]
        for j in range(3):
            for k in range(steps):
                rows = pl.ds(k * depth, depth)
                at = first + 3 + j * steps + k
                groups.append([fetch(w_hbm.at[j, rows], w_ref.at[j, rows], at)])
        groups[first].append(fetch(t_hbm, t_ref, first + 2))
        stream = Stream(groups, 8)

        def put(first, sig, rows):
            n = rows.shape[0] // BLOCK
            core, chip = first // 256, first % 256 // BLOCK
            o_ref[chip : chip + n, core, sig * BLOCK : (sig + 1) * BLOCK, :] = rows.astype(BF16).reshape(
                n, BLOCK, SEQ_DEV
            )

        for i in range(512 // gate):
            stream.wait(i)
            put(i * gate, 3, dot(ow_ref[i * gate : (i + 1) * gate], g_ref[...], NT))
        for c in range(2):
            put(c * 256, 4, f_ref[:, c * 256 : (c + 1) * 256].T)
        for chip in range(8):
            lanes = pl.ds(pl.multiple_of(chip * 512 + y_ref[0] * 128, 128), 128)
            o_ref[chip, 1, 5 * BLOCK :, :] = g_ref[:, lanes]
        for j in range(3):
            total = None
            for k in range(steps):
                stream.wait(first + j * steps + k)
                part = dot(t_ref[:, k * depth : (k + 1) * depth], w_ref[j, k * depth : (k + 1) * depth])
                total = part if total is None else total + part
            if j == 0:
                for chip in range(8):
                    lanes = pl.ds(pl.multiple_of(chip * 512 + y_ref[0] * 128, 128), 128)
                    o_ref[chip, 0, 5 * BLOCK :, :] = t_ref[:, lanes]
            for c in range(2):
                put(c * 256, j, total[:, c * 256 : (c + 1) * 256].T)

    vm = pl.BlockSpec(memory_space=pltpu.VMEM)
    hbm = pl.BlockSpec(memory_space=pl.ANY)
    return call(
        kernel,
        in_specs=[pl.BlockSpec(memory_space=pltpu.SMEM)] + [hbm] * 5,
        out_specs=vm,
        out_shape=jax.ShapeDtypeStruct((8, 2, 5 * BLOCK + 128, SEQ_DEV), BF16),
        scratch_shapes=[
            pltpu.VMEM((SEQ_DEV, 512), F32),
            pltpu.VMEM((SEQ_DEV, 4096), BF16),
            pltpu.VMEM((SEQ_DEV, 4096), BF16),
            pltpu.VMEM((3, 4096, 512), BF16),
            pltpu.VMEM((512, 4096), BF16),
            pltpu.SemaphoreType.DMA((3 + 512 // gate + 3 * steps,)),
        ],
        flops=2 * 128 * 4096 * 2048,
        bytes_accessed=19 * MIB,
        vmem=28,
        name="project",
    )(quarter, in_hbm(tokens), in_hbm(out_grad), in_hbm(filters), in_hbm(weight), in_hbm(out_weight))


def cosine_matrix():
    odd = 2 * np.arange(SEQ, dtype=np.int64) + 1
    turns = np.outer(odd, odd) % (8 * SEQ)
    return np.cos(turns * (2.0 * np.pi / (8 * SEQ))).astype(ml_dtypes.bfloat16)


def frequency_rows():
    half = (2 * np.arange(SEQ) + 1) * (np.pi / (4 * SEQ))
    sign = 1.0 - 2.0 * (np.arange(SEQ) % 2)
    rows = np.zeros((8, SEQ), np.float32)
    rows[0], rows[1], rows[2] = np.cos(half), np.sin(half), sign
    return rows


def convolve(received, matrix, rows, flip):
    chunk = 512
    n_chunks = SEQ // chunk

    def kernel(r_ref, m_ref, w_ref, j_ref, b_ref, o_ref, c_ref, x_ref, y_ref):
        rev = j_ref[...]
        c_ref[...] = r_ref[:, 5 * BLOCK :, :].reshape(8, 2, SEQ_DEV, 128)
        for b in range(16):
            part = r_ref[b]
            key, value = part[32:64].astype(F32), part[64:96].astype(F32)
            query, gate = part[0:32].astype(F32), part[96:128].astype(F32)
            lanes = pl.ds(b * 128, 128)
            x_ref[0:32, lanes] = part[128:160]
            x_ref[32:64, lanes] = (key * value).astype(BF16)
            x_ref[64:96, lanes] = (gate * query).astype(BF16)
        for b in range(8):
            x_ref[96:192, pl.ds((7 - b) * 256, 256)] = dot(x_ref[0:96, pl.ds(b * 256, 256)], rev).astype(BF16)
        for n in range(n_chunks):
            lanes = pl.ds(n * chunk, chunk)
            spec = dot(x_ref[...], m_ref[:, lanes])
            wr, wi, sign = w_ref[0:1, lanes], w_ref[1:2, lanes], w_ref[2:3, lanes]
            hr, mr, gr = spec[0:32], spec[32:64], spec[64:96]
            neg = -sign
            hi, mi, gi = spec[96:128] * neg, spec[128:160] * neg, spec[160:192] * neg
            hwr, hwi = hr * wr - hi * wi, hr * wi + hi * wr
            mwr, mwi = mr * wr - mi * wi, mr * wi + mi * wr
            y_ref[0:32, lanes] = (hwr * mr - hwi * mi).astype(BF16)
            y_ref[32:64, lanes] = (gr * hwr + gi * hwi).astype(BF16)
            y_ref[64:96, lanes] = (gr * mwr + gi * mwi).astype(BF16)
            imag = jnp.concatenate(
                [hwr * mi + hwi * mr, gi * hwr - gr * hwi, gi * mwr - gr * mwi], axis=0
            ).astype(BF16)
            for b in range(chunk // 256):
                at = SEQ - (n * chunk + (b + 1) * 256)
                y_ref[96:192, pl.ds(at, 256)] = dot(imag[:, b * 256 : (b + 1) * 256], rev).astype(BF16)
        scale = 1.0 / SEQ
        for n in range(n_chunks):
            lanes = pl.ds(n * chunk, chunk)
            back = dot(y_ref[...], m_ref[:, lanes])
            back = (back[0:96] - back[96:192] * w_ref[2:3, lanes]) * scale
            for b in range(chunk // 128):
                at = n * (chunk // 128) + b
                part = r_ref[at]
                cut = slice(b * 128, (b + 1) * 128)
                conv, mixed, raw = back[0:32, cut], back[32:64, cut], back[64:96, cut]
                query, key, value, gate = (part[32 * i : 32 * i + 32].astype(F32) for i in range(4))
                gq = (gate * conv).astype(BF16)
                gk = (mixed * value).astype(BF16)
                gv = (mixed * key).astype(BF16)
                pos = pl.ds((at % 2 * 8 + at // 2) * 128, 128)
                b_ref[0:32, pos] = gq
                b_ref[32:64, pos] = gk
                b_ref[64:96, pos] = gv
                b_ref[96:128, pos] = (query * conv).astype(BF16)
                o_ref[at, 0:32, :] = gq
                o_ref[at, 32:64, :] = gk
                o_ref[at, 64:96, :] = gv
                raw = raw * (1.0 / math.sqrt(SEQ))
                high = raw.astype(BF16)
                o_ref[at, 96:128, :] = high
                o_ref[at, 128:160, :] = (raw - high.astype(F32)).astype(BF16)

    vm = pl.BlockSpec(memory_space=pltpu.VMEM)
    return call(
        kernel,
        in_specs=[vm, vm, vm, vm],
        out_specs=[vm, vm, vm],
        out_shape=[
            jax.ShapeDtypeStruct((128, SEQ), BF16),
            jax.ShapeDtypeStruct((16, 160, 128), BF16),
            jax.ShapeDtypeStruct((8, 2, SEQ_DEV, 128), BF16),
        ],
        scratch_shapes=[
            pltpu.VMEM((192, SEQ), BF16),
            pltpu.VMEM((192, SEQ), BF16),
        ],
        flops=4 * 192 * SEQ * SEQ,
        bytes_accessed=12 * MIB,
        vmem=20,
        name="convolve",
    )(received, in_vmem(matrix), rows, flip)


def input_partial(received, weight):
    steps = 8
    depth = 4096 // steps

    def kernel(r_ref, w_hbm, o_ref, f_ref, w_ref, g_ref, sem):
        groups = []
        for s in range(steps):
            rows = pl.ds(s * depth, depth)
            groups.append(
                [
                    pltpu.make_async_copy(w_hbm.at[j, rows], w_ref.at[rows, pl.ds(j * 512, 512)], sem.at[s, j])
                    for j in range(3)
                ]
            )
        stream = Stream(groups, steps)
        for chip in range(8):
            for core in range(2):
                at = core * 256 + chip * BLOCK
                for j in range(5):
                    g_ref[j * 512 + at : j * 512 + at + BLOCK, :] = r_ref[
                        2 * chip + core, j * BLOCK : (j + 1) * BLOCK, :
                    ]
        grads = g_ref[0:1536].astype(F32).T.astype(BF16)
        f_ref[...] = (g_ref[1536:2048].astype(F32) + g_ref[2048:2560].astype(F32)).T
        for s in range(steps):
            stream.wait(s)
            o_ref[s] = dot(grads, w_ref[s * depth : (s + 1) * depth], NT).astype(BF16)

    vm = pl.BlockSpec(memory_space=pltpu.VMEM)
    return call(
        kernel,
        in_specs=[vm, pl.BlockSpec(memory_space=pl.ANY)],
        out_specs=[vm, vm],
        out_shape=[
            jax.ShapeDtypeStruct((8, SEQ_DEV, 512), BF16),
            jax.ShapeDtypeStruct((SEQ_DEV, 512), F32),
        ],
        scratch_shapes=[
            pltpu.VMEM((4096, 1536), BF16),
            pltpu.VMEM((2560, SEQ_DEV), BF16),
            pltpu.SemaphoreType.DMA((steps, 3)),
        ],
        flops=2 * 128 * 4096 * 1536,
        bytes_accessed=14 * MIB,
        vmem=24,
        name="input_partial",
    )(received, in_hbm(weight))


def sum_partials(parts):
    def kernel(p_ref, o_ref):
        total = p_ref[0].astype(F32)
        for i in range(1, 8):
            total = total + p_ref[i].astype(F32)
        o_ref[...] = total.astype(BF16)

    vm = pl.BlockSpec(memory_space=pltpu.VMEM)
    return call(
        kernel,
        in_specs=[vm],
        out_specs=vm,
        out_shape=jax.ShapeDtypeStruct((SEQ_DEV, 512), BF16),
        bytes_accessed=MIB,
        name="sum_partials",
    )(parts)


def pair(first, second, third, fourth):
    def kernel(a, b, c, d, o_ref, p_ref, sem):
        copies = []
        for i, (src, out) in enumerate(((a, o_ref), (b, o_ref), (c, p_ref), (d, p_ref))):
            copies.append(pltpu.make_async_copy(src, out.at[pl.ds(i % 2 * 128, 128)], sem.at[i]))
        for copy in copies:
            copy.start()
        for copy in copies:
            copy.wait()

    hbm = pl.BlockSpec(memory_space=pl.ANY)
    return call(
        kernel,
        in_specs=[hbm] * 4,
        out_specs=[pl.BlockSpec(memory_space=pltpu.VMEM)] * 2,
        out_shape=[jax.ShapeDtypeStruct((256, SEQ), BF16)] * 2,
        scratch_shapes=[pltpu.SemaphoreType.DMA((4,))],
        vmem=4,
        name="pair",
    )(first, second, third, fourth)


def gather_columns(place_ref, column_refs, t_ref, t_sem):
    core = place_ref[8]
    copies = []
    for i in range(8):
        lanes = pl.ds(pl.multiple_of(place_ref[9 + i % 4] * 128, 128), 128)
        kind = core if i < 4 else 1 - core
        for c in range(2):
            src = column_refs[i].at[:, c]
            copies.append(pltpu.make_async_copy(src, t_ref.at[kind, c, :, :, lanes], t_sem.at[c, i]))
    return copies


def gather_blocks(block_refs, first_rows, g_ref, sem):
    copies = [[], [], [], []]
    for j in range(4):
        for k in range(4):
            src = block_refs[k].at[pl.ds(first_rows[k] + j * BLOCK, BLOCK)]
            copies[j].append(pltpu.make_async_copy(src, g_ref.at[j, pl.ds(k * BLOCK, BLOCK)], sem.at[j, k]))
    return copies


COLUMN_SCRATCH = (
    pltpu.VMEM((2, 2, 8, SEQ_DEV, 512), BF16),
    pltpu.VMEM((4, 128, SEQ), BF16),
    pltpu.SemaphoreType.DMA((2, 8)),
    pltpu.SemaphoreType.DMA((4, 4)),
)


def first_products(place, columns, blocks):
    first_rows = [first for _, first in blocks]

    def kernel(place_ref, *refs):
        o_ref, t_hbm, t_ref, g_ref, t_sem, sem, out_sem = refs[12:]
        t_copies = gather_columns(place_ref, refs[:8], t_ref, t_sem)
        copies = gather_blocks(refs[8:12], first_rows, g_ref, sem)
        for copy in t_copies + copies[0] + copies[1] + copies[2] + copies[3]:
            copy.start()
        for j in range(4):
            for copy in copies[j] + (t_copies if j == 0 else []):
                copy.wait()
            if j == 0:
                keep = pltpu.make_async_copy(t_ref, t_hbm, out_sem)
                keep.start()
            o_ref[j] = dot(g_ref[j], t_ref[j // 3].reshape(SEQ, 512))
        keep.wait()

    hbm = pl.BlockSpec(memory_space=pl.ANY)
    return call(
        kernel,
        in_specs=[pl.BlockSpec(memory_space=pltpu.SMEM)] + [hbm] * 12,
        out_specs=[pl.BlockSpec(memory_space=pltpu.VMEM), hbm],
        out_shape=[
            jax.ShapeDtypeStruct((4, 128, 512), F32),
            jax.ShapeDtypeStruct((2, 2, 8, SEQ_DEV, 512), BF16),
        ],
        scratch_shapes=list(COLUMN_SCRATCH) + [pltpu.SemaphoreType.DMA],
        vmem=16,
        name="first_products",
    )(place, columns[0], *map(in_hbm, columns[1:]), blocks[0][0], *[in_hbm(block) for block, _ in blocks[1:]])


def weight_gradients(place, columns, products, blocks):
    factor = 1.0 / math.sqrt(SEQ)
    first_rows = [first for _, first in blocks]

    def kernel(place_ref, p_ref, *refs):
        t_hbm, in_hbm, out_hbm, send_ref, t_ref, g_ref, t_sem, sem, all_ref, res_ref, out_sem = refs[4:]
        core = place_ref[8]
        t_copies = [pltpu.make_async_copy(t_hbm.at[i], t_ref.at[i], t_sem.at[i, 0]) for i in range(2)]
        copies = gather_blocks(refs[:4], first_rows, g_ref, sem)
        for copy in [t_copies[0]] + copies[0] + copies[1] + copies[2] + [t_copies[1]] + copies[3]:
            copy.start()
        half = pl.multiple_of(core * 256, 256)
        rest = pl.multiple_of((1 - core) * 256, 256)
        for j in range(4):
            for k in range(4):
                at = pl.multiple_of(place_ref[k] * BLOCK, BLOCK)
                all_ref[j, pl.ds(at, BLOCK), :] = p_ref[j, k * BLOCK : (k + 1) * BLOCK, :]
        outs = []
        for j in range(4):
            for copy in copies[j] + ([t_copies[j // 3]] if j % 3 == 0 else []):
                copy.wait()
            more = dot(g_ref[j], t_ref[j // 3].reshape(SEQ, 512))
            for k in range(4):
                at = pl.multiple_of(place_ref[4 + k] * BLOCK, BLOCK)
                all_ref[j, pl.ds(at, BLOCK), :] = more[k * BLOCK : (k + 1) * BLOCK]
            total = all_ref[j] * factor
            if j < 3:
                res_ref[j] = total.T
                send_ref[j * 256 : (j + 1) * 256, :] = res_ref[j, pl.ds(rest, 256), :].astype(BF16)
                src, dst = res_ref.at[j, pl.ds(half, 256)], in_hbm.at[j, :, pl.ds(half, 256)]
            else:
                res_ref[3, 0:256] = total[:, 0:256]
                res_ref[3, 256:512] = total[:, 256:512]
                send_ref[768:1024, :] = res_ref[3, pl.ds(rest, 256), :].astype(BF16)
                src, dst = res_ref.at[3, pl.ds(half, 256)], out_hbm.at[pl.ds(half, 256)]
            outs.append(pltpu.make_async_copy(src, dst, out_sem.at[j]))
            outs[-1].start()
        for copy in outs:
            copy.wait()

    vm = pl.BlockSpec(memory_space=pltpu.VMEM)
    hbm = pl.BlockSpec(memory_space=pl.ANY)
    return call(
        kernel,
        in_specs=[pl.BlockSpec(memory_space=pltpu.SMEM), vm] + [hbm] * 5,
        out_specs=[hbm, hbm, vm],
        out_shape=[
            jax.ShapeDtypeStruct((3, 256, 512), F32),
            jax.ShapeDtypeStruct((512, 256), F32),
            jax.ShapeDtypeStruct((1024, 256), BF16),
        ],
        scratch_shapes=list(COLUMN_SCRATCH)
        + [
            pltpu.VMEM((4, 256, 512), F32),
            pltpu.VMEM((4, 512, 256), F32),
            pltpu.SemaphoreType.DMA((4,)),
        ],
        vmem=24,
        name="weight_gradients",
    )(place, products, *[in_hbm(block) for block, _ in blocks], in_hbm(columns))


def fill_halves(place, sent, in_grad, out_grad):
    def kernel(place_ref, s_ref, in_old, out_old, in_hbm, out_hbm, res_ref, sem):
        half = pl.multiple_of((1 - place_ref[8]) * 256, 256)
        outs = []
        for j in range(4):
            res_ref[j] = s_ref[j * 256 : (j + 1) * 256, :].astype(F32)
            dst = in_hbm.at[j, :, pl.ds(half, 256)] if j < 3 else out_hbm.at[pl.ds(half, 256)]
            outs.append(pltpu.make_async_copy(res_ref.at[j], dst, sem.at[j]))
            outs[-1].start()
        for copy in outs:
            copy.wait()

    vm = pl.BlockSpec(memory_space=pltpu.VMEM)
    hbm = pl.BlockSpec(memory_space=pl.ANY)
    return call(
        kernel,
        in_specs=[pl.BlockSpec(memory_space=pltpu.SMEM), vm, hbm, hbm],
        out_specs=[hbm, hbm],
        out_shape=[jax.ShapeDtypeStruct((3, 256, 512), F32), jax.ShapeDtypeStruct((512, 256), F32)],
        scratch_shapes=[pltpu.VMEM((4, 256, 256), F32), pltpu.SemaphoreType.DMA((4,))],
        input_output_aliases={2: 0, 3: 1},
        vmem=8,
        name="fill_halves",
    )(place, sent, in_hbm(in_grad), in_hbm(out_grad))


def chip_hop(x_flip, z_step):
    pairs = []
    for i in range(16):
        x, z, core = i // 8, i // 2 % 4, i % 2
        pairs.append((i, ((x ^ x_flip) * 4 + (z + z_step) % 4) * 2 + core))
    return pairs


def swap_cores(value):
    return lax.ppermute(value, "ctx", [(i, i ^ 1) for i in range(16)])


def swap(pieces, axis, groups=None):
    return lax.all_to_all(pieces, axis, 0, 0, axis_index_groups=groups, tiled=True)


HOPS = ((0, 0), (0, 1), (0, 3), (1, 0), (0, 2), (1, 1), (1, 3), (1, 2))


def hop(value, x_flip, z_step):
    return lax.ppermute(value, "ctx", chip_hop(x_flip, z_step))


def after(value, *others):
    return lax.optimization_barrier((value,) + others)[0]


def hop_y(value, step):
    return lax.ppermute(value, "mp", [(i, i // 4 * 4 + (i % 4 + step) % 4) for i in range(8)])


def on_device(tokens, out_grad, in_weight, out_weight, filters):
    position = lax.axis_index("ctx")
    core, x, z = position & 1, position >> 3, (position >> 1) & 3
    y = lax.axis_index("mp") & 3
    place = [((x ^ f) << 2) + ((z - s) & 3) for f, s in HOPS] + [core] + [(y - s) & 3 for s in (0, 1, 3, 2)]
    place = jnp.stack(place).astype(jnp.int32)
    weight = jnp.transpose(in_weight, (1, 0, 2))
    signals = project(y.astype(jnp.int32)[None], tokens, out_grad, weight, out_weight, filters)
    signals = swap(signals.reshape(16, 5 * BLOCK + 128, SEQ_DEV), "ctx")
    flip = jnp.asarray(np.eye(256)[::-1].astype(ml_dtypes.bfloat16))
    block, pieces, columns = convolve(
        signals, jnp.asarray(cosine_matrix()), jnp.asarray(frequency_rows()), flip
    )
    columns = [columns] + [hop_y(columns, s) for s in (1, 3, 2)]
    up, down, flipped = hop(block, 0, 1), hop(block, 0, 3), hop(block, 1, 0)
    pieces = swap(pieces, "ctx")
    up, down, flipped, pieces = lax.optimization_barrier((up, down, flipped, pieces))
    near, here = pair(up, down, block, flipped)
    across, two = hop(near, 1, 0), hop(here, 0, 2)
    pieces = after(pieces, near)
    partial, filter_grad = input_partial(pieces, weight)
    parts = swap(partial, "mp")
    columns = columns[:2] + [after(value, partial) for value in columns[2:]]
    columns += [swap_cores(value) for value in columns]
    input_grad = sum_partials(parts)
    blocks = [(block, 0), (up, 0), (down, 0), (flipped, 0), (two, 0), (across, 0), (across, 128), (two, 128)]
    products, columns = first_products(place, columns, blocks[:4])
    in_grad, out_weight_grad, send = weight_gradients(place, columns, products, blocks[4:])
    in_grad, out_weight_grad = fill_halves(place, swap_cores(send), in_grad, out_weight_grad)
    return (input_grad, jnp.transpose(in_grad, (1, 0, 2)), out_weight_grad, filter_grad)


def solution(mesh):
    in_specs = (P("ctx", None), P("ctx", None), P(None, None, "mp"), P("mp", None), P("ctx", "mp"))
    out_specs = (P("ctx", "mp"), P("ctx", None, "mp"), P("mp", "ctx"), P("ctx", "mp"))
    return jax.shard_map(
        on_device, mesh=mesh, in_specs=in_specs, out_specs=out_specs, check_vma=False
    )
```

```python
import math

import jax
import jax.numpy as jnp
import ml_dtypes
import numpy as np
from jax import lax
from jax.experimental import pallas as pl
from jax.experimental.pallas import tpu as pltpu
from jax.sharding import PartitionSpec as P

F32 = jnp.float32
BF16 = jnp.bfloat16
NT = (((1,), (1,)), ((), ()))
NN = (((1,), (0,)), ((), ()))
MIB = 1 << 20
BLOCK = 32
SEQ_DEV = 128
SEQ = 2048


def dot(a, b, dims=NN):
    return lax.dot_general(a, b, dims, preferred_element_type=F32)


def in_hbm(value):
    return pltpu.with_memory_space_constraint(value, pltpu.HBM)


def in_vmem(value):
    return pltpu.with_memory_space_constraint(value, pltpu.VMEM)


class Stream:
    def __init__(self, groups, ahead):
        self.groups, self.started, self.ahead = groups, 0, ahead
        self.start(ahead)

    def start(self, upto):
        while self.started < min(upto, len(self.groups)):
            for copy in self.groups[self.started]:
                copy.start()
            self.started += 1

    def wait(self, index):
        for copy in self.groups[index]:
            copy.wait()
        self.start(index + 1 + self.ahead)


def call(kernel, *, flops=0, bytes_accessed=0, vmem=32, **kw):
    return pl.pallas_call(
        kernel,
        compiler_params=pltpu.CompilerParams(vmem_limit_bytes=vmem * MIB),
        cost_estimate=pl.CostEstimate(flops=flops, bytes_accessed=bytes_accessed, transcendentals=0),
        **kw,
    )


def project(quarter, tokens, out_grad, weight, out_weight, filters):
    depth = 2048
    steps = 4096 // depth
    gate = 256

    def kernel(y_ref, t_hbm, g_hbm, f_hbm, w_hbm, ow_hbm, o_ref, f_ref, t_ref, g_ref, w_ref, ow_ref, sem):
        def fetch(src, dst, at):
            return pltpu.make_async_copy(src, dst, sem.at[at])

        gates = [pl.ds(gate * i, gate) for i in range(512 // gate)]
        groups = [[fetch(ow_hbm.at[rows], ow_ref.at[rows], i)] for i, rows in enumerate(gates)]
        first = len(groups)
        groups[0] = [fetch(f_hbm, f_ref, first), fetch(g_hbm, g_ref, first + 1)] + groups[0]
        for j in range(3):
            for k in range(steps):
                rows = pl.ds(k * depth, depth)
                at = first + 3 + j * steps + k
                groups.append([fetch(w_hbm.at[j, rows], w_ref.at[j, rows], at)])
        groups[first].append(fetch(t_hbm, t_ref, first + 2))
        stream = Stream(groups, 8)

        def put(first, sig, rows):
            n = rows.shape[0] // BLOCK
            core, chip = first // 256, first % 256 // BLOCK
            o_ref[chip : chip + n, core, sig * BLOCK : (sig + 1) * BLOCK, :] = rows.astype(BF16).reshape(
                n, BLOCK, SEQ_DEV
            )

        for i in range(512 // gate):
            stream.wait(i)
            put(i * gate, 3, dot(ow_ref[i * gate : (i + 1) * gate], g_ref[...], NT))
        for c in range(2):
            put(c * 256, 4, f_ref[:, c * 256 : (c + 1) * 256].T)
        for chip in range(8):
            lanes = pl.ds(pl.multiple_of(chip * 512 + y_ref[0] * 128, 128), 128)
            o_ref[chip, 1, 5 * BLOCK :, :] = g_ref[:, lanes]
        for j in range(3):
            total = None
            for k in range(steps):
                stream.wait(first + j * steps + k)
                part = dot(t_ref[:, k * depth : (k + 1) * depth], w_ref[j, k * depth : (k + 1) * depth])
                total = part if total is None else total + part
            if j == 0:
                for chip in range(8):
                    lanes = pl.ds(pl.multiple_of(chip * 512 + y_ref[0] * 128, 128), 128)
                    o_ref[chip, 0, 5 * BLOCK :, :] = t_ref[:, lanes]
            for c in range(2):
                put(c * 256, j, total[:, c * 256 : (c + 1) * 256].T)

    vm = pl.BlockSpec(memory_space=pltpu.VMEM)
    hbm = pl.BlockSpec(memory_space=pl.ANY)
    return call(
        kernel,
        in_specs=[pl.BlockSpec(memory_space=pltpu.SMEM)] + [hbm] * 5,
        out_specs=vm,
        out_shape=jax.ShapeDtypeStruct((8, 2, 5 * BLOCK + 128, SEQ_DEV), BF16),
        scratch_shapes=[
            pltpu.VMEM((SEQ_DEV, 512), F32),
            pltpu.VMEM((SEQ_DEV, 4096), BF16),
            pltpu.VMEM((SEQ_DEV, 4096), BF16),
            pltpu.VMEM((3, 4096, 512), BF16),
            pltpu.VMEM((512, 4096), BF16),
            pltpu.SemaphoreType.DMA((3 + 512 // gate + 3 * steps,)),
        ],
        flops=2 * 128 * 4096 * 2048,
        bytes_accessed=19 * MIB,
        vmem=28,
        name="project",
    )(quarter, in_hbm(tokens), in_hbm(out_grad), in_hbm(filters), in_hbm(weight), in_hbm(out_weight))


def cosine_matrix():
    odd = 2 * np.arange(SEQ, dtype=np.int64) + 1
    turns = np.outer(odd, odd) % (8 * SEQ)
    return np.cos(turns * (2.0 * np.pi / (8 * SEQ))).astype(ml_dtypes.bfloat16)


def frequency_rows():
    half = (2 * np.arange(SEQ) + 1) * (np.pi / (4 * SEQ))
    sign = 1.0 - 2.0 * (np.arange(SEQ) % 2)
    rows = np.zeros((8, SEQ), np.float32)
    rows[0], rows[1], rows[2] = np.cos(half), np.sin(half), sign
    return rows


def convolve(received, matrix, rows, flip):
    chunk = 256
    n_chunks = SEQ // chunk

    def kernel(r_ref, m_ref, w_ref, j_ref, b_ref, o_ref, c_ref, x_ref, y_ref):
        rev = j_ref[...]
        c_ref[...] = r_ref[:, 5 * BLOCK :, :].reshape(8, 2, SEQ_DEV, 128)
        for b in range(16):
            part = r_ref[b]
            key, value = part[32:64].astype(F32), part[64:96].astype(F32)
            query, gate = part[0:32].astype(F32), part[96:128].astype(F32)
            lanes = pl.ds(b * 128, 128)
            x_ref[0:32, lanes] = part[128:160]
            x_ref[32:64, lanes] = (key * value).astype(BF16)
            x_ref[64:96, lanes] = (gate * query).astype(BF16)
        for b in range(8):
            x_ref[96:192, pl.ds((7 - b) * 256, 256)] = dot(x_ref[0:96, pl.ds(b * 256, 256)], rev).astype(BF16)
        for n in range(n_chunks):
            lanes = pl.ds(n * chunk, chunk)
            spec = dot(x_ref[...], m_ref[:, lanes])
            wr, wi, sign = w_ref[0:1, lanes], w_ref[1:2, lanes], w_ref[2:3, lanes]
            hr, mr, gr = spec[0:32], spec[32:64], spec[64:96]
            neg = -sign
            hi, mi, gi = spec[96:128] * neg, spec[128:160] * neg, spec[160:192] * neg
            hwr, hwi = hr * wr - hi * wi, hr * wi + hi * wr
            mwr, mwi = mr * wr - mi * wi, mr * wi + mi * wr
            y_ref[0:32, lanes] = (hwr * mr - hwi * mi).astype(BF16)
            y_ref[32:64, lanes] = (gr * hwr + gi * hwi).astype(BF16)
            y_ref[64:96, lanes] = (gr * mwr + gi * mwi).astype(BF16)
            imag = jnp.concatenate(
                [hwr * mi + hwi * mr, gi * hwr - gr * hwi, gi * mwr - gr * mwi], axis=0
            ).astype(BF16)
            for b in range(chunk // 256):
                at = SEQ - (n * chunk + (b + 1) * 256)
                y_ref[96:192, pl.ds(at, 256)] = dot(imag[:, b * 256 : (b + 1) * 256], rev).astype(BF16)
        scale = 1.0 / SEQ
        for n in range(n_chunks):
            lanes = pl.ds(n * chunk, chunk)
            back = dot(y_ref[...], m_ref[:, lanes])
            back = (back[0:96] - back[96:192] * w_ref[2:3, lanes]) * scale
            for b in range(chunk // 128):
                at = n * (chunk // 128) + b
                part = r_ref[at]
                cut = slice(b * 128, (b + 1) * 128)
                conv, mixed, raw = back[0:32, cut], back[32:64, cut], back[64:96, cut]
                query, key, value, gate = (part[32 * i : 32 * i + 32].astype(F32) for i in range(4))
                gq = (gate * conv).astype(BF16)
                gk = (mixed * value).astype(BF16)
                gv = (mixed * key).astype(BF16)
                pos = pl.ds((at % 2 * 8 + at // 2) * 128, 128)
                b_ref[0:32, pos] = gq
                b_ref[32:64, pos] = gk
                b_ref[64:96, pos] = gv
                b_ref[96:128, pos] = (query * conv).astype(BF16)
                o_ref[at, 0:32, :] = gq
                o_ref[at, 32:64, :] = gk
                o_ref[at, 64:96, :] = gv
                raw = raw * (1.0 / math.sqrt(SEQ))
                high = raw.astype(BF16)
                o_ref[at, 96:128, :] = high
                o_ref[at, 128:160, :] = (raw - high.astype(F32)).astype(BF16)

    vm = pl.BlockSpec(memory_space=pltpu.VMEM)
    return call(
        kernel,
        in_specs=[vm, vm, vm, vm],
        out_specs=[vm, vm, vm],
        out_shape=[
            jax.ShapeDtypeStruct((128, SEQ), BF16),
            jax.ShapeDtypeStruct((16, 160, 128), BF16),
            jax.ShapeDtypeStruct((8, 2, SEQ_DEV, 128), BF16),
        ],
        scratch_shapes=[
            pltpu.VMEM((192, SEQ), BF16),
            pltpu.VMEM((192, SEQ), BF16),
        ],
        flops=4 * 192 * SEQ * SEQ,
        bytes_accessed=12 * MIB,
        vmem=20,
        name="convolve",
    )(received, in_vmem(matrix), rows, flip)


def input_partial(received, weight):
    steps = 8
    depth = 4096 // steps

    def kernel(r_ref, w_hbm, o_ref, f_ref, w_ref, g_ref, sem):
        groups = []
        for s in range(steps):
            rows = pl.ds(s * depth, depth)
            groups.append(
                [
                    pltpu.make_async_copy(w_hbm.at[j, rows], w_ref.at[rows, pl.ds(j * 512, 512)], sem.at[s, j])
                    for j in range(3)
                ]
            )
        stream = Stream(groups, steps)
        for chip in range(8):
            for core in range(2):
                at = core * 256 + chip * BLOCK
                for j in range(5):
                    g_ref[j * 512 + at : j * 512 + at + BLOCK, :] = r_ref[
                        2 * chip + core, j * BLOCK : (j + 1) * BLOCK, :
                    ]
        grads = g_ref[0:1536].astype(F32).T.astype(BF16)
        f_ref[...] = (g_ref[1536:2048].astype(F32) + g_ref[2048:2560].astype(F32)).T
        for s in range(steps):
            stream.wait(s)
            o_ref[s] = dot(grads, w_ref[s * depth : (s + 1) * depth], NT).astype(BF16)

    vm = pl.BlockSpec(memory_space=pltpu.VMEM)
    return call(
        kernel,
        in_specs=[vm, pl.BlockSpec(memory_space=pl.ANY)],
        out_specs=[vm, vm],
        out_shape=[
            jax.ShapeDtypeStruct((8, SEQ_DEV, 512), BF16),
            jax.ShapeDtypeStruct((SEQ_DEV, 512), F32),
        ],
        scratch_shapes=[
            pltpu.VMEM((4096, 1536), BF16),
            pltpu.VMEM((2560, SEQ_DEV), BF16),
            pltpu.SemaphoreType.DMA((steps, 3)),
        ],
        flops=2 * 128 * 4096 * 1536,
        bytes_accessed=14 * MIB,
        vmem=24,
        name="input_partial",
    )(received, in_hbm(weight))


def sum_partials(parts):
    def kernel(p_ref, o_ref):
        total = p_ref[0].astype(F32)
        for i in range(1, 8):
            total = total + p_ref[i].astype(F32)
        o_ref[...] = total.astype(BF16)

    vm = pl.BlockSpec(memory_space=pltpu.VMEM)
    return call(
        kernel,
        in_specs=[vm],
        out_specs=vm,
        out_shape=jax.ShapeDtypeStruct((SEQ_DEV, 512), BF16),
        bytes_accessed=MIB,
        name="sum_partials",
    )(parts)


def pair(first, second, third, fourth):
    def kernel(a, b, c, d, o_ref, p_ref, sem):
        copies = []
        for i, (src, out) in enumerate(((a, o_ref), (b, o_ref), (c, p_ref), (d, p_ref))):
            copies.append(pltpu.make_async_copy(src, out.at[pl.ds(i % 2 * 128, 128)], sem.at[i]))
        for copy in copies:
            copy.start()
        for copy in copies:
            copy.wait()

    hbm = pl.BlockSpec(memory_space=pl.ANY)
    return call(
        kernel,
        in_specs=[hbm] * 4,
        out_specs=[pl.BlockSpec(memory_space=pltpu.VMEM)] * 2,
        out_shape=[jax.ShapeDtypeStruct((256, SEQ), BF16)] * 2,
        scratch_shapes=[pltpu.SemaphoreType.DMA((4,))],
        vmem=4,
        name="pair",
    )(first, second, third, fourth)


def gather_columns(place_ref, column_refs, t_ref, t_sem):
    core = place_ref[8]
    copies = []
    for i in range(8):
        lanes = pl.ds(pl.multiple_of(place_ref[9 + i % 4] * 128, 128), 128)
        kind = core if i < 4 else 1 - core
        for c in range(2):
            src = column_refs[i].at[:, c]
            copies.append(pltpu.make_async_copy(src, t_ref.at[kind, c, :, :, lanes], t_sem.at[c, i]))
    return copies


def gather_blocks(block_refs, first_rows, g_ref, sem):
    copies = [[], [], [], []]
    for j in range(4):
        for k in range(4):
            src = block_refs[k].at[pl.ds(first_rows[k] + j * BLOCK, BLOCK)]
            copies[j].append(pltpu.make_async_copy(src, g_ref.at[j, pl.ds(k * BLOCK, BLOCK)], sem.at[j, k]))
    return copies


COLUMN_SCRATCH = (
    pltpu.VMEM((2, 2, 8, SEQ_DEV, 512), BF16),
    pltpu.VMEM((4, 128, SEQ), BF16),
    pltpu.SemaphoreType.DMA((2, 8)),
    pltpu.SemaphoreType.DMA((4, 4)),
)


def first_products(place, columns, blocks):
    first_rows = [first for _, first in blocks]

    def kernel(place_ref, *refs):
        o_ref, t_hbm, t_ref, g_ref, t_sem, sem, out_sem = refs[12:]
        t_copies = gather_columns(place_ref, refs[:8], t_ref, t_sem)
        copies = gather_blocks(refs[8:12], first_rows, g_ref, sem)
        for copy in t_copies + copies[0] + copies[1] + copies[2] + copies[3]:
            copy.start()
        for j in range(4):
            for copy in copies[j] + (t_copies if j == 0 else []):
                copy.wait()
            if j == 0:
                keep = pltpu.make_async_copy(t_ref, t_hbm, out_sem)
                keep.start()
            o_ref[j] = dot(g_ref[j], t_ref[j // 3].reshape(SEQ, 512))
        keep.wait()

    hbm = pl.BlockSpec(memory_space=pl.ANY)
    return call(
        kernel,
        in_specs=[pl.BlockSpec(memory_space=pltpu.SMEM)] + [hbm] * 12,
        out_specs=[pl.BlockSpec(memory_space=pltpu.VMEM), hbm],
        out_shape=[
            jax.ShapeDtypeStruct((4, 128, 512), F32),
            jax.ShapeDtypeStruct((2, 2, 8, SEQ_DEV, 512), BF16),
        ],
        scratch_shapes=list(COLUMN_SCRATCH) + [pltpu.SemaphoreType.DMA],
        vmem=16,
        name="first_products",
    )(place, columns[0], *map(in_hbm, columns[1:]), blocks[0][0], *[in_hbm(block) for block, _ in blocks[1:]])


def weight_gradients(place, columns, products, blocks):
    factor = 1.0 / math.sqrt(SEQ)
    first_rows = [first for _, first in blocks]

    def kernel(place_ref, p_ref, *refs):
        t_hbm, in_hbm, out_hbm, send_ref, t_ref, g_ref, t_sem, sem, all_ref, res_ref, out_sem = refs[4:]
        core = place_ref[8]
        t_copies = [pltpu.make_async_copy(t_hbm.at[i], t_ref.at[i], t_sem.at[i, 0]) for i in range(2)]
        copies = gather_blocks(refs[:4], first_rows, g_ref, sem)
        for copy in [t_copies[0]] + copies[0] + copies[1] + copies[2] + [t_copies[1]] + copies[3]:
            copy.start()
        half = pl.multiple_of(core * 256, 256)
        rest = pl.multiple_of((1 - core) * 256, 256)
        for j in range(4):
            for k in range(4):
                at = pl.multiple_of(place_ref[k] * BLOCK, BLOCK)
                all_ref[j, pl.ds(at, BLOCK), :] = p_ref[j, k * BLOCK : (k + 1) * BLOCK, :]
        outs = []
        for j in range(4):
            for copy in copies[j] + ([t_copies[j // 3]] if j % 3 == 0 else []):
                copy.wait()
            more = dot(g_ref[j], t_ref[j // 3].reshape(SEQ, 512))
            for k in range(4):
                at = pl.multiple_of(place_ref[4 + k] * BLOCK, BLOCK)
                all_ref[j, pl.ds(at, BLOCK), :] = more[k * BLOCK : (k + 1) * BLOCK]
            total = all_ref[j] * factor
            if j < 3:
                res_ref[j] = total.T
                send_ref[j * 256 : (j + 1) * 256, :] = res_ref[j, pl.ds(rest, 256), :].astype(BF16)
                src, dst = res_ref.at[j, pl.ds(half, 256)], in_hbm.at[j, :, pl.ds(half, 256)]
            else:
                res_ref[3, 0:256] = total[:, 0:256]
                res_ref[3, 256:512] = total[:, 256:512]
                send_ref[768:1024, :] = res_ref[3, pl.ds(rest, 256), :].astype(BF16)
                src, dst = res_ref.at[3, pl.ds(half, 256)], out_hbm.at[pl.ds(half, 256)]
            outs.append(pltpu.make_async_copy(src, dst, out_sem.at[j]))
            outs[-1].start()
        for copy in outs:
            copy.wait()

    vm = pl.BlockSpec(memory_space=pltpu.VMEM)
    hbm = pl.BlockSpec(memory_space=pl.ANY)
    return call(
        kernel,
        in_specs=[pl.BlockSpec(memory_space=pltpu.SMEM), vm] + [hbm] * 5,
        out_specs=[hbm, hbm, vm],
        out_shape=[
            jax.ShapeDtypeStruct((3, 256, 512), F32),
            jax.ShapeDtypeStruct((512, 256), F32),
            jax.ShapeDtypeStruct((1024, 256), BF16),
        ],
        scratch_shapes=list(COLUMN_SCRATCH)
        + [
            pltpu.VMEM((4, 256, 512), F32),
            pltpu.VMEM((4, 512, 256), F32),
            pltpu.SemaphoreType.DMA((4,)),
        ],
        vmem=24,
        name="weight_gradients",
    )(place, products, *[in_hbm(block) for block, _ in blocks], in_hbm(columns))


def fill_halves(place, sent, in_grad, out_grad):
    def kernel(place_ref, s_ref, in_old, out_old, in_hbm, out_hbm, res_ref, sem):
        half = pl.multiple_of((1 - place_ref[8]) * 256, 256)
        outs = []
        for j in range(4):
            res_ref[j] = s_ref[j * 256 : (j + 1) * 256, :].astype(F32)
            dst = in_hbm.at[j, :, pl.ds(half, 256)] if j < 3 else out_hbm.at[pl.ds(half, 256)]
            outs.append(pltpu.make_async_copy(res_ref.at[j], dst, sem.at[j]))
            outs[-1].start()
        for copy in outs:
            copy.wait()

    vm = pl.BlockSpec(memory_space=pltpu.VMEM)
    hbm = pl.BlockSpec(memory_space=pl.ANY)
    return call(
        kernel,
        in_specs=[pl.BlockSpec(memory_space=pltpu.SMEM), vm, hbm, hbm],
        out_specs=[hbm, hbm],
        out_shape=[jax.ShapeDtypeStruct((3, 256, 512), F32), jax.ShapeDtypeStruct((512, 256), F32)],
        scratch_shapes=[pltpu.VMEM((4, 256, 256), F32), pltpu.SemaphoreType.DMA((4,))],
        input_output_aliases={2: 0, 3: 1},
        vmem=8,
        name="fill_halves",
    )(place, sent, in_hbm(in_grad), in_hbm(out_grad))


def chip_hop(x_flip, z_step):
    pairs = []
    for i in range(16):
        x, z, core = i // 8, i // 2 % 4, i % 2
        pairs.append((i, ((x ^ x_flip) * 4 + (z + z_step) % 4) * 2 + core))
    return pairs


def swap_cores(value):
    return lax.ppermute(value, "ctx", [(i, i ^ 1) for i in range(16)])


def swap(pieces, axis, groups=None):
    return lax.all_to_all(pieces, axis, 0, 0, axis_index_groups=groups, tiled=True)


HOPS = ((0, 0), (0, 1), (0, 3), (1, 0), (0, 2), (1, 1), (1, 3), (1, 2))


def hop(value, x_flip, z_step):
    return lax.ppermute(value, "ctx", chip_hop(x_flip, z_step))


def after(value, *others):
    return lax.optimization_barrier((value,) + others)[0]


def hop_y(value, step):
    return lax.ppermute(value, "mp", [(i, i // 4 * 4 + (i % 4 + step) % 4) for i in range(8)])


def on_device(tokens, out_grad, in_weight, out_weight, filters):
    position = lax.axis_index("ctx")
    core, x, z = position & 1, position >> 3, (position >> 1) & 3
    y = lax.axis_index("mp") & 3
    place = [((x ^ f) << 2) + ((z - s) & 3) for f, s in HOPS] + [core] + [(y - s) & 3 for s in (0, 1, 3, 2)]
    place = jnp.stack(place).astype(jnp.int32)
    weight = jnp.transpose(in_weight, (1, 0, 2))
    signals = project(y.astype(jnp.int32)[None], tokens, out_grad, weight, out_weight, filters)
    signals = swap(signals.reshape(16, 5 * BLOCK + 128, SEQ_DEV), "ctx")
    flip = jnp.asarray(np.eye(256)[::-1].astype(ml_dtypes.bfloat16))
    block, pieces, columns = convolve(
        signals, jnp.asarray(cosine_matrix()), jnp.asarray(frequency_rows()), flip
    )
    columns = [columns] + [hop_y(columns, s) for s in (1, 3, 2)]
    up, down, flipped = hop(block, 0, 1), hop(block, 0, 3), hop(block, 1, 0)
    pieces = swap(pieces, "ctx")
    up, down, flipped, pieces = lax.optimization_barrier((up, down, flipped, pieces))
    near, here = pair(up, down, block, flipped)
    across, two = hop(near, 1, 0), hop(here, 0, 2)
    pieces = after(pieces, near)
    partial, filter_grad = input_partial(pieces, weight)
    parts = swap(partial, "mp")
    columns = columns[:2] + [after(value, partial) for value in columns[2:]]
    columns += [swap_cores(value) for value in columns]
    input_grad = sum_partials(parts)
    blocks = [(block, 0), (up, 0), (down, 0), (flipped, 0), (two, 0), (across, 0), (across, 128), (two, 128)]
    products, columns = first_products(place, columns, blocks[:4])
    in_grad, out_weight_grad, send = weight_gradients(place, columns, products, blocks[4:])
    in_grad, out_weight_grad = fill_halves(place, swap_cores(send), in_grad, out_weight_grad)
    return (input_grad, jnp.transpose(in_grad, (1, 0, 2)), out_weight_grad, filter_grad)


def solution(mesh):
    in_specs = (P("ctx", None), P("ctx", None), P(None, None, "mp"), P("mp", None), P("ctx", "mp"))
    out_specs = (P("ctx", "mp"), P("ctx", None, "mp"), P("mp", "ctx"), P("ctx", "mp"))
    return jax.shard_map(
        on_device, mesh=mesh, in_specs=in_specs, out_specs=out_specs, check_vma=False
    )
```

```python
import math

import jax
import jax.numpy as jnp
import ml_dtypes
import numpy as np
from jax import lax
from jax.experimental import pallas as pl
from jax.experimental.pallas import tpu as pltpu
from jax.sharding import PartitionSpec as P

F32 = jnp.float32
BF16 = jnp.bfloat16
NT = (((1,), (1,)), ((), ()))
NN = (((1,), (0,)), ((), ()))
MIB = 1 << 20
BLOCK = 32
SEQ_DEV = 128
SEQ = 2048


def dot(a, b, dims=NN):
    return lax.dot_general(a, b, dims, preferred_element_type=F32)


def in_hbm(value):
    return pltpu.with_memory_space_constraint(value, pltpu.HBM)


def in_vmem(value):
    return pltpu.with_memory_space_constraint(value, pltpu.VMEM)


class Stream:
    def __init__(self, groups, ahead):
        self.groups, self.started, self.ahead = groups, 0, ahead
        self.start(ahead)

    def start(self, upto):
        while self.started < min(upto, len(self.groups)):
            for copy in self.groups[self.started]:
                copy.start()
            self.started += 1

    def wait(self, index):
        for copy in self.groups[index]:
            copy.wait()
        self.start(index + 1 + self.ahead)


def call(kernel, *, flops=0, bytes_accessed=0, vmem=32, **kw):
    return pl.pallas_call(
        kernel,
        compiler_params=pltpu.CompilerParams(vmem_limit_bytes=vmem * MIB),
        cost_estimate=pl.CostEstimate(flops=flops, bytes_accessed=bytes_accessed, transcendentals=0),
        **kw,
    )


def project(quarter, tokens, out_grad, weight, out_weight, filters):
    depth = 2048
    steps = 4096 // depth
    gate = 256

    def kernel(y_ref, t_hbm, g_hbm, f_hbm, w_hbm, ow_hbm, o_ref, f_ref, t_ref, g_ref, w_ref, ow_ref, sem):
        def fetch(src, dst, at):
            return pltpu.make_async_copy(src, dst, sem.at[at])

        gates = [pl.ds(gate * i, gate) for i in range(512 // gate)]
        groups = [[fetch(ow_hbm.at[rows], ow_ref.at[rows], i)] for i, rows in enumerate(gates)]
        first = len(groups)
        groups[0] = [fetch(f_hbm, f_ref, first), fetch(g_hbm, g_ref, first + 1)] + groups[0]
        for j in range(3):
            for k in range(steps):
                rows = pl.ds(k * depth, depth)
                at = first + 3 + j * steps + k
                groups.append([fetch(w_hbm.at[j, rows], w_ref.at[j, rows], at)])
        groups[first].append(fetch(t_hbm, t_ref, first + 2))
        stream = Stream(groups, 8)

        def put(first, sig, rows):
            n = rows.shape[0] // BLOCK
            core, chip = first // 256, first % 256 // BLOCK
            o_ref[chip : chip + n, core, sig * BLOCK : (sig + 1) * BLOCK, :] = rows.astype(BF16).reshape(
                n, BLOCK, SEQ_DEV
            )

        for i in range(512 // gate):
            stream.wait(i)
            put(i * gate, 3, dot(ow_ref[i * gate : (i + 1) * gate], g_ref[...], NT))
        for c in range(2):
            put(c * 256, 4, f_ref[:, c * 256 : (c + 1) * 256].T)
        for chip in range(8):
            lanes = pl.ds(pl.multiple_of(chip * 512 + y_ref[0] * 128, 128), 128)
            o_ref[chip, 1, 5 * BLOCK :, :] = g_ref[:, lanes]
        for j in range(3):
            total = None
            for k in range(steps):
                stream.wait(first + j * steps + k)
                part = dot(t_ref[:, k * depth : (k + 1) * depth], w_ref[j, k * depth : (k + 1) * depth])
                total = part if total is None else total + part
            if j == 0:
                for chip in range(8):
                    lanes = pl.ds(pl.multiple_of(chip * 512 + y_ref[0] * 128, 128), 128)
                    o_ref[chip, 0, 5 * BLOCK :, :] = t_ref[:, lanes]
            for c in range(2):
                put(c * 256, j, total[:, c * 256 : (c + 1) * 256].T)

    vm = pl.BlockSpec(memory_space=pltpu.VMEM)
    hbm = pl.BlockSpec(memory_space=pl.ANY)
    return call(
        kernel,
        in_specs=[pl.BlockSpec(memory_space=pltpu.SMEM)] + [hbm] * 5,
        out_specs=vm,
        out_shape=jax.ShapeDtypeStruct((8, 2, 5 * BLOCK + 128, SEQ_DEV), BF16),
        scratch_shapes=[
            pltpu.VMEM((SEQ_DEV, 512), F32),
            pltpu.VMEM((SEQ_DEV, 4096), BF16),
            pltpu.VMEM((SEQ_DEV, 4096), BF16),
            pltpu.VMEM((3, 4096, 512), BF16),
            pltpu.VMEM((512, 4096), BF16),
            pltpu.SemaphoreType.DMA((3 + 512 // gate + 3 * steps,)),
        ],
        flops=2 * 128 * 4096 * 2048,
        bytes_accessed=19 * MIB,
        vmem=28,
        name="project",
    )(quarter, in_hbm(tokens), in_hbm(out_grad), in_hbm(filters), in_hbm(weight), in_hbm(out_weight))


def cosine_matrix():
    odd = 2 * np.arange(SEQ, dtype=np.int64) + 1
    turns = np.outer(odd, odd) % (8 * SEQ)
    return np.cos(turns * (2.0 * np.pi / (8 * SEQ))).astype(ml_dtypes.bfloat16)


def frequency_rows():
    half = (2 * np.arange(SEQ) + 1) * (np.pi / (4 * SEQ))
    sign = 1.0 - 2.0 * (np.arange(SEQ) % 2)
    rows = np.zeros((8, SEQ), np.float32)
    rows[0], rows[1], rows[2] = np.cos(half), np.sin(half), sign
    return rows


def convolve(received, matrix, rows, flip):
    chunk = 1024
    n_chunks = SEQ // chunk

    def kernel(r_ref, m_ref, w_ref, j_ref, b_ref, o_ref, c_ref, x_ref, y_ref):
        rev = j_ref[...]
        c_ref[...] = r_ref[:, 5 * BLOCK :, :].reshape(8, 2, SEQ_DEV, 128)
        for b in range(16):
            part = r_ref[b]
            key, value = part[32:64].astype(F32), part[64:96].astype(F32)
            query, gate = part[0:32].astype(F32), part[96:128].astype(F32)
            lanes = pl.ds(b * 128, 128)
            x_ref[0:32, lanes] = part[128:160]
            x_ref[32:64, lanes] = (key * value).astype(BF16)
            x_ref[64:96, lanes] = (gate * query).astype(BF16)
        for b in range(8):
            x_ref[96:192, pl.ds((7 - b) * 256, 256)] = dot(x_ref[0:96, pl.ds(b * 256, 256)], rev).astype(BF16)
        for n in range(n_chunks):
            lanes = pl.ds(n * chunk, chunk)
            spec = dot(x_ref[...], m_ref[:, lanes])
            wr, wi, sign = w_ref[0:1, lanes], w_ref[1:2, lanes], w_ref[2:3, lanes]
            hr, mr, gr = spec[0:32], spec[32:64], spec[64:96]
            neg = -sign
            hi, mi, gi = spec[96:128] * neg, spec[128:160] * neg, spec[160:192] * neg
            hwr, hwi = hr * wr - hi * wi, hr * wi + hi * wr
            mwr, mwi = mr * wr - mi * wi, mr * wi + mi * wr
            y_ref[0:32, lanes] = (hwr * mr - hwi * mi).astype(BF16)
            y_ref[32:64, lanes] = (gr * hwr + gi * hwi).astype(BF16)
            y_ref[64:96, lanes] = (gr * mwr + gi * mwi).astype(BF16)
            imag = jnp.concatenate(
                [hwr * mi + hwi * mr, gi * hwr - gr * hwi, gi * mwr - gr * mwi], axis=0
            ).astype(BF16)
            for b in range(chunk // 256):
                at = SEQ - (n * chunk + (b + 1) * 256)
                y_ref[96:192, pl.ds(at, 256)] = dot(imag[:, b * 256 : (b + 1) * 256], rev).astype(BF16)
        scale = 1.0 / SEQ
        for n in range(n_chunks):
            lanes = pl.ds(n * chunk, chunk)
            back = dot(y_ref[...], m_ref[:, lanes])
            back = (back[0:96] - back[96:192] * w_ref[2:3, lanes]) * scale
            for b in range(chunk // 128):
                at = n * (chunk // 128) + b
                part = r_ref[at]
                cut = slice(b * 128, (b + 1) * 128)
                conv, mixed, raw = back[0:32, cut], back[32:64, cut], back[64:96, cut]
                query, key, value, gate = (part[32 * i : 32 * i + 32].astype(F32) for i in range(4))
                gq = (gate * conv).astype(BF16)
                gk = (mixed * value).astype(BF16)
                gv = (mixed * key).astype(BF16)
                pos = pl.ds((at % 2 * 8 + at // 2) * 128, 128)
                b_ref[0:32, pos] = gq
                b_ref[32:64, pos] = gk
                b_ref[64:96, pos] = gv
                b_ref[96:128, pos] = (query * conv).astype(BF16)
                o_ref[at, 0:32, :] = gq
                o_ref[at, 32:64, :] = gk
                o_ref[at, 64:96, :] = gv
                raw = raw * (1.0 / math.sqrt(SEQ))
                high = raw.astype(BF16)
                o_ref[at, 96:128, :] = high
                o_ref[at, 128:160, :] = (raw - high.astype(F32)).astype(BF16)

    vm = pl.BlockSpec(memory_space=pltpu.VMEM)
    return call(
        kernel,
        in_specs=[vm, vm, vm, vm],
        out_specs=[vm, vm, vm],
        out_shape=[
            jax.ShapeDtypeStruct((128, SEQ), BF16),
            jax.ShapeDtypeStruct((16, 160, 128), BF16),
            jax.ShapeDtypeStruct((8, 2, SEQ_DEV, 128), BF16),
        ],
        scratch_shapes=[
            pltpu.VMEM((192, SEQ), BF16),
            pltpu.VMEM((192, SEQ), BF16),
        ],
        flops=4 * 192 * SEQ * SEQ,
        bytes_accessed=12 * MIB,
        vmem=20,
        name="convolve",
    )(received, in_vmem(matrix), rows, flip)


def input_partial(received, weight):
    steps = 8
    depth = 4096 // steps

    def kernel(r_ref, w_hbm, o_ref, f_ref, w_ref, g_ref, sem):
        groups = []
        for s in range(steps):
            rows = pl.ds(s * depth, depth)
            groups.append(
                [
                    pltpu.make_async_copy(w_hbm.at[j, rows], w_ref.at[rows, pl.ds(j * 512, 512)], sem.at[s, j])
                    for j in range(3)
                ]
            )
        stream = Stream(groups, steps)
        for chip in range(8):
            for core in range(2):
                at = core * 256 + chip * BLOCK
                for j in range(5):
                    g_ref[j * 512 + at : j * 512 + at + BLOCK, :] = r_ref[
                        2 * chip + core, j * BLOCK : (j + 1) * BLOCK, :
                    ]
        grads = g_ref[0:1536].astype(F32).T.astype(BF16)
        f_ref[...] = (g_ref[1536:2048].astype(F32) + g_ref[2048:2560].astype(F32)).T
        for s in range(steps):
            stream.wait(s)
            o_ref[s] = dot(grads, w_ref[s * depth : (s + 1) * depth], NT).astype(BF16)

    vm = pl.BlockSpec(memory_space=pltpu.VMEM)
    return call(
        kernel,
        in_specs=[vm, pl.BlockSpec(memory_space=pl.ANY)],
        out_specs=[vm, vm],
        out_shape=[
            jax.ShapeDtypeStruct((8, SEQ_DEV, 512), BF16),
            jax.ShapeDtypeStruct((SEQ_DEV, 512), F32),
        ],
        scratch_shapes=[
            pltpu.VMEM((4096, 1536), BF16),
            pltpu.VMEM((2560, SEQ_DEV), BF16),
            pltpu.SemaphoreType.DMA((steps, 3)),
        ],
        flops=2 * 128 * 4096 * 1536,
        bytes_accessed=14 * MIB,
        vmem=24,
        name="input_partial",
    )(received, in_hbm(weight))


def sum_partials(parts):
    def kernel(p_ref, o_ref):
        total = p_ref[0].astype(F32)
        for i in range(1, 8):
            total = total + p_ref[i].astype(F32)
        o_ref[...] = total.astype(BF16)

    vm = pl.BlockSpec(memory_space=pltpu.VMEM)
    return call(
        kernel,
        in_specs=[vm],
        out_specs=vm,
        out_shape=jax.ShapeDtypeStruct((SEQ_DEV, 512), BF16),
        bytes_accessed=MIB,
        name="sum_partials",
    )(parts)


def pair(first, second, third, fourth):
    def kernel(a, b, c, d, o_ref, p_ref, sem):
        copies = []
        for i, (src, out) in enumerate(((a, o_ref), (b, o_ref), (c, p_ref), (d, p_ref))):
            copies.append(pltpu.make_async_copy(src, out.at[pl.ds(i % 2 * 128, 128)], sem.at[i]))
        for copy in copies:
            copy.start()
        for copy in copies:
            copy.wait()

    hbm = pl.BlockSpec(memory_space=pl.ANY)
    return call(
        kernel,
        in_specs=[hbm] * 4,
        out_specs=[pl.BlockSpec(memory_space=pltpu.VMEM)] * 2,
        out_shape=[jax.ShapeDtypeStruct((256, SEQ), BF16)] * 2,
        scratch_shapes=[pltpu.SemaphoreType.DMA((4,))],
        vmem=4,
        name="pair",
    )(first, second, third, fourth)


def gather_columns(place_ref, column_refs, t_ref, t_sem):
    core = place_ref[8]
    copies = []
    for i in range(8):
        lanes = pl.ds(pl.multiple_of(place_ref[9 + i % 4] * 128, 128), 128)
        kind = core if i < 4 else 1 - core
        for c in range(2):
            src = column_refs[i].at[:, c]
            copies.append(pltpu.make_async_copy(src, t_ref.at[kind, c, :, :, lanes], t_sem.at[c, i]))
    return copies


def gather_blocks(block_refs, first_rows, g_ref, sem):
    copies = [[], [], [], []]
    for j in range(4):
        for k in range(4):
            src = block_refs[k].at[pl.ds(first_rows[k] + j * BLOCK, BLOCK)]
            copies[j].append(pltpu.make_async_copy(src, g_ref.at[j, pl.ds(k * BLOCK, BLOCK)], sem.at[j, k]))
    return copies


COLUMN_SCRATCH = (
    pltpu.VMEM((2, 2, 8, SEQ_DEV, 512), BF16),
    pltpu.VMEM((4, 128, SEQ), BF16),
    pltpu.SemaphoreType.DMA((2, 8)),
    pltpu.SemaphoreType.DMA((4, 4)),
)


def first_products(place, columns, blocks):
    first_rows = [first for _, first in blocks]

    def kernel(place_ref, *refs):
        o_ref, t_hbm, t_ref, g_ref, t_sem, sem, out_sem = refs[12:]
        t_copies = gather_columns(place_ref, refs[:8], t_ref, t_sem)
        copies = gather_blocks(refs[8:12], first_rows, g_ref, sem)
        for copy in t_copies + copies[0] + copies[1] + copies[2] + copies[3]:
            copy.start()
        for j in range(4):
            for copy in copies[j] + (t_copies if j == 0 else []):
                copy.wait()
            if j == 0:
                keep = pltpu.make_async_copy(t_ref, t_hbm, out_sem)
                keep.start()
            o_ref[j] = dot(g_ref[j], t_ref[j // 3].reshape(SEQ, 512))
        keep.wait()

    hbm = pl.BlockSpec(memory_space=pl.ANY)
    return call(
        kernel,
        in_specs=[pl.BlockSpec(memory_space=pltpu.SMEM)] + [hbm] * 12,
        out_specs=[pl.BlockSpec(memory_space=pltpu.VMEM), hbm],
        out_shape=[
            jax.ShapeDtypeStruct((4, 128, 512), F32),
            jax.ShapeDtypeStruct((2, 2, 8, SEQ_DEV, 512), BF16),
        ],
        scratch_shapes=list(COLUMN_SCRATCH) + [pltpu.SemaphoreType.DMA],
        vmem=16,
        name="first_products",
    )(place, columns[0], *map(in_hbm, columns[1:]), blocks[0][0], *[in_hbm(block) for block, _ in blocks[1:]])


def weight_gradients(place, columns, products, blocks):
    factor = 1.0 / math.sqrt(SEQ)
    first_rows = [first for _, first in blocks]

    def kernel(place_ref, p_ref, *refs):
        t_hbm, in_hbm, out_hbm, send_ref, t_ref, g_ref, t_sem, sem, all_ref, res_ref, out_sem = refs[4:]
        core = place_ref[8]
        t_copies = [pltpu.make_async_copy(t_hbm.at[i], t_ref.at[i], t_sem.at[i, 0]) for i in range(2)]
        copies = gather_blocks(refs[:4], first_rows, g_ref, sem)
        for copy in [t_copies[0]] + copies[0] + copies[1] + copies[2] + [t_copies[1]] + copies[3]:
            copy.start()
        half = pl.multiple_of(core * 256, 256)
        rest = pl.multiple_of((1 - core) * 256, 256)
        for j in range(4):
            for k in range(4):
                at = pl.multiple_of(place_ref[k] * BLOCK, BLOCK)
                all_ref[j, pl.ds(at, BLOCK), :] = p_ref[j, k * BLOCK : (k + 1) * BLOCK, :]
        outs = []
        for j in range(4):
            for copy in copies[j] + ([t_copies[j // 3]] if j % 3 == 0 else []):
                copy.wait()
            more = dot(g_ref[j], t_ref[j // 3].reshape(SEQ, 512))
            for k in range(4):
                at = pl.multiple_of(place_ref[4 + k] * BLOCK, BLOCK)
                all_ref[j, pl.ds(at, BLOCK), :] = more[k * BLOCK : (k + 1) * BLOCK]
            total = all_ref[j] * factor
            if j < 3:
                res_ref[j] = total.T
                send_ref[j * 256 : (j + 1) * 256, :] = res_ref[j, pl.ds(rest, 256), :].astype(BF16)
                src, dst = res_ref.at[j, pl.ds(half, 256)], in_hbm.at[j, :, pl.ds(half, 256)]
            else:
                res_ref[3, 0:256] = total[:, 0:256]
                res_ref[3, 256:512] = total[:, 256:512]
                send_ref[768:1024, :] = res_ref[3, pl.ds(rest, 256), :].astype(BF16)
                src, dst = res_ref.at[3, pl.ds(half, 256)], out_hbm.at[pl.ds(half, 256)]
            outs.append(pltpu.make_async_copy(src, dst, out_sem.at[j]))
            outs[-1].start()
        for copy in outs:
            copy.wait()

    vm = pl.BlockSpec(memory_space=pltpu.VMEM)
    hbm = pl.BlockSpec(memory_space=pl.ANY)
    return call(
        kernel,
        in_specs=[pl.BlockSpec(memory_space=pltpu.SMEM), vm] + [hbm] * 5,
        out_specs=[hbm, hbm, vm],
        out_shape=[
            jax.ShapeDtypeStruct((3, 256, 512), F32),
            jax.ShapeDtypeStruct((512, 256), F32),
            jax.ShapeDtypeStruct((1024, 256), BF16),
        ],
        scratch_shapes=list(COLUMN_SCRATCH)
        + [
            pltpu.VMEM((4, 256, 512), F32),
            pltpu.VMEM((4, 512, 256), F32),
            pltpu.SemaphoreType.DMA((4,)),
        ],
        vmem=24,
        name="weight_gradients",
    )(place, products, *[in_hbm(block) for block, _ in blocks], in_hbm(columns))


def fill_halves(place, sent, in_grad, out_grad):
    def kernel(place_ref, s_ref, in_old, out_old, in_hbm, out_hbm, res_ref, sem):
        half = pl.multiple_of((1 - place_ref[8]) * 256, 256)
        outs = []
        for j in range(4):
            res_ref[j] = s_ref[j * 256 : (j + 1) * 256, :].astype(F32)
            dst = in_hbm.at[j, :, pl.ds(half, 256)] if j < 3 else out_hbm.at[pl.ds(half, 256)]
            outs.append(pltpu.make_async_copy(res_ref.at[j], dst, sem.at[j]))
            outs[-1].start()
        for copy in outs:
            copy.wait()

    vm = pl.BlockSpec(memory_space=pltpu.VMEM)
    hbm = pl.BlockSpec(memory_space=pl.ANY)
    return call(
        kernel,
        in_specs=[pl.BlockSpec(memory_space=pltpu.SMEM), vm, hbm, hbm],
        out_specs=[hbm, hbm],
        out_shape=[jax.ShapeDtypeStruct((3, 256, 512), F32), jax.ShapeDtypeStruct((512, 256), F32)],
        scratch_shapes=[pltpu.VMEM((4, 256, 256), F32), pltpu.SemaphoreType.DMA((4,))],
        input_output_aliases={2: 0, 3: 1},
        vmem=8,
        name="fill_halves",
    )(place, sent, in_hbm(in_grad), in_hbm(out_grad))


def chip_hop(x_flip, z_step):
    pairs = []
    for i in range(16):
        x, z, core = i // 8, i // 2 % 4, i % 2
        pairs.append((i, ((x ^ x_flip) * 4 + (z + z_step) % 4) * 2 + core))
    return pairs


def swap_cores(value):
    return lax.ppermute(value, "ctx", [(i, i ^ 1) for i in range(16)])


def swap(pieces, axis, groups=None):
    return lax.all_to_all(pieces, axis, 0, 0, axis_index_groups=groups, tiled=True)


HOPS = ((0, 0), (0, 1), (0, 3), (1, 0), (0, 2), (1, 1), (1, 3), (1, 2))


def hop(value, x_flip, z_step):
    return lax.ppermute(value, "ctx", chip_hop(x_flip, z_step))


def after(value, *others):
    return lax.optimization_barrier((value,) + others)[0]


def hop_y(value, step):
    return lax.ppermute(value, "mp", [(i, i // 4 * 4 + (i % 4 + step) % 4) for i in range(8)])


def on_device(tokens, out_grad, in_weight, out_weight, filters):
    position = lax.axis_index("ctx")
    core, x, z = position & 1, position >> 3, (position >> 1) & 3
    y = lax.axis_index("mp") & 3
    place = [((x ^ f) << 2) + ((z - s) & 3) for f, s in HOPS] + [core] + [(y - s) & 3 for s in (0, 1, 3, 2)]
    place = jnp.stack(place).astype(jnp.int32)
    weight = jnp.transpose(in_weight, (1, 0, 2))
    signals = project(y.astype(jnp.int32)[None], tokens, out_grad, weight, out_weight, filters)
    signals = swap(signals.reshape(16, 5 * BLOCK + 128, SEQ_DEV), "ctx")
    flip = jnp.asarray(np.eye(256)[::-1].astype(ml_dtypes.bfloat16))
    block, pieces, columns = convolve(
        signals, jnp.asarray(cosine_matrix()), jnp.asarray(frequency_rows()), flip
    )
    columns = [columns] + [hop_y(columns, s) for s in (1, 3, 2)]
    up, down, flipped = hop(block, 0, 1), hop(block, 0, 3), hop(block, 1, 0)
    pieces = swap(pieces, "ctx")
    up, down, flipped, pieces = lax.optimization_barrier((up, down, flipped, pieces))
    near, here = pair(up, down, block, flipped)
    across, two = hop(near, 1, 0), hop(here, 0, 2)
    pieces = after(pieces, near)
    partial, filter_grad = input_partial(pieces, weight)
    parts = swap(partial, "mp")
    columns = columns[:2] + [after(value, partial) for value in columns[2:]]
    columns += [swap_cores(value) for value in columns]
    input_grad = sum_partials(parts)
    blocks = [(block, 0), (up, 0), (down, 0), (flipped, 0), (two, 0), (across, 0), (across, 128), (two, 128)]
    products, columns = first_products(place, columns, blocks[:4])
    in_grad, out_weight_grad, send = weight_gradients(place, columns, products, blocks[4:])
    in_grad, out_weight_grad = fill_halves(place, swap_cores(send), in_grad, out_weight_grad)
    return (input_grad, jnp.transpose(in_grad, (1, 0, 2)), out_weight_grad, filter_grad)


def solution(mesh):
    in_specs = (P("ctx", None), P("ctx", None), P(None, None, "mp"), P("mp", None), P("ctx", "mp"))
    out_specs = (P("ctx", "mp"), P("ctx", None, "mp"), P("mp", "ctx"), P("ctx", "mp"))
    return jax.shard_map(
        on_device, mesh=mesh, in_specs=in_specs, out_specs=out_specs, check_vma=False
    )
```
